32 devices in a mesh: ctx: 2 (over y), tp: 4 (over x, core), section: 4 (over z).
Axes of the slice: x: 2, y: 2, z: 4, core: 2. Of those that a mesh axis runs over, the one named last changes fastest.
Arguments:
- queries: bfloat16 [2, 1024, 8192], P(None, ('ctx', 'section'), 'tp'), may hold values from -15 to 15
- self_kv: bfloat16 [2, 1024, 2048], P(None, ('ctx', 'section')), may hold values from -6 to 6
- image_kv: bfloat16 [32, 2048], P(('ctx', 'tp', 'section')), may hold values from -6 to 6
- cross_gate: float32 [64], P('tp'), may hold values from 0.3 to 2
- lengths: int32 [2], replicated, may hold values from 256 to 1024, as said below
Outputs:
- attended: bfloat16 [2, 1024, 8192], P(None, ('ctx', 'section'), 'tp')
The draws below stay inside these ranges and needn't reach their ends.
Inputs may be any that keep to these rules, and one draw needn't show every extreme that they name: `lengths`: one of the two sequences uses all 1024 positions, the other fewer.
All inputs are finite; a program needn't handle non-finite values.
Results may differ from the reference program's by a relative error of at most 0.004.
Values may be sent and summed in bfloat16 or wider, within the bound.
No kernel may reach another device: no remote copies, remote signals or barrier semaphores. Data moves between devices by JAX's collectives and lax.ppermute only.
A program may use at most 128 MiB of HBM per device.

```python
import math
import jax
import jax.numpy as jnp
from jax import lax

HQ = 64
KVH = 8
HEAD_SIZE = 128
SEQ_LEN = 1024
IMG_TOKENS = 32


def unit_noise(key, shape):
    return jnp.clip(jax.random.normal(key, shape, jnp.float32), -6.0, 6.0)


def draw_queries(key, part):
    base = 2.5 * unit_noise(jax.random.fold_in(key, 1), (2, SEQ_LEN, HQ, HEAD_SIZE))
    return base.reshape(2, SEQ_LEN, HQ * HEAD_SIZE).astype(jnp.bfloat16)


def draw_self_kv(key, part):
    base = unit_noise(jax.random.fold_in(key, 4), (2, SEQ_LEN, KVH, 2, HEAD_SIZE))
    return base.reshape(2, SEQ_LEN, KVH * 2 * HEAD_SIZE).astype(jnp.bfloat16)


def draw_image_kv(key, part):
    base = unit_noise(jax.random.fold_in(key, 5), (IMG_TOKENS, KVH, 2, HEAD_SIZE))
    return base.reshape(IMG_TOKENS, KVH * 2 * HEAD_SIZE).astype(jnp.bfloat16)


def draw_lengths(key, part):
    full_index = jax.random.randint(jax.random.fold_in(key, 21), (), 0, 2)
    shorter = jax.random.randint(jax.random.fold_in(key, 22), (), SEQ_LEN // 4, SEQ_LEN)
    slots = jnp.arange(2, dtype=jnp.int32)
    return jnp.where(slots == full_index, SEQ_LEN, shorter).astype(jnp.int32)


def block_levels(rng, extent, pieces, smallest, largest):
    def one(dim, blocks):
        heights = jax.random.uniform(jax.random.fold_in(jax.random.fold_in(rng, 6), dim), (blocks,), jnp.float32, smallest / len(pieces), largest / len(pieces))
        return jnp.repeat(jnp.exp(heights), extent[dim] // blocks).reshape((-1,) + (1,) * (len(extent) - dim - 1))

    loudness = one(*pieces[0])
    for cut in pieces[1:]:
        loudness = loudness * one(*cut)
    return loudness


def setup_inputs(seed: int = 0) -> dict:
    seeds = jax.random.split(jax.random.key(seed), 6)
    queries = draw_queries(jax.random.fold_in(seeds[5], 71), 0)
    self_kv = draw_self_kv(jax.random.fold_in(seeds[5], 71), 0)
    image_kv = draw_image_kv(jax.random.fold_in(seeds[5], 71), 0)
    cross_gate = jnp.clip(0.3 + 1.7 * jax.random.uniform(seeds[3], (HQ,), jnp.float32) ** block_levels(seeds[3], (HQ,), ((0, 4),), -0.2, 0.2), 0.3, 2.0)
    lengths = draw_lengths(jax.random.fold_in(seeds[5], 71), 0)
    return dict(queries=queries, self_kv=self_kv, image_kv=image_kv, cross_gate=cross_gate, lengths=lengths)


neg_large = -1e+30

def attend(query_matrix, key_matrix, value_matrix, allowed):
    logit_scores = jnp.einsum('hnz,hfz->hnf', query_matrix.astype(jnp.float32), key_matrix.astype(jnp.float32)) * (1.0 / math.sqrt(HEAD_SIZE))
    masked = jnp.where(allowed, logit_scores, neg_large)
    row_best = lax.optimization_barrier(jnp.max(masked, axis=-1, keepdims=True))
    weights = jnp.where(allowed, jnp.exp(masked - row_best), 0.0)
    row_total = lax.optimization_barrier(jnp.sum(weights, axis=-1, keepdims=True))
    rounded_scores = weights.astype(jnp.bfloat16)
    summed_output = jnp.einsum('eug,egr->eur', rounded_scores.astype(jnp.float32), value_matrix.astype(jnp.float32))
    return summed_output / row_total

def reference(queries, self_kv, image_kv, cross_gate, lengths):
    seq_len = queries.shape[1]
    image_rows = image_kv.shape[0]
    heads_per_group = HQ // KVH
    head_queries = jnp.transpose(queries.reshape(2, seq_len, HQ, HEAD_SIZE), (2, 0, 1, 3))
    kv_pairs = self_kv.reshape(2, seq_len, KVH, 2, HEAD_SIZE)
    self_keys = jnp.transpose(kv_pairs[:, :, :, 0], (2, 0, 1, 3))
    self_values = jnp.transpose(kv_pairs[:, :, :, 1], (2, 0, 1, 3))
    image_pairs = image_kv.reshape(image_rows, KVH, 2, HEAD_SIZE)
    image_keys = jnp.transpose(image_pairs[:, :, 0], (1, 0, 2))
    image_values = jnp.transpose(image_pairs[:, :, 1], (1, 0, 2))
    position = jnp.arange(seq_len, dtype=jnp.int32)
    allowed = (position[None, None, :] <= position[None, :, None]) & (position[None, None, :] < lengths.astype(jnp.int32)[:, None, None])
    everywhere = jnp.ones((1, 1, 1), jnp.bool_)

    def one_head(head_index):
        kv_index = head_index // heads_per_group
        query_one = lax.dynamic_index_in_dim(head_queries, head_index, 0, keepdims=False)
        key_one = lax.dynamic_index_in_dim(self_keys, kv_index, 0, keepdims=False)
        value_one = lax.dynamic_index_in_dim(self_values, kv_index, 0, keepdims=False)
        self_out = attend(query_one, key_one, value_one, allowed)
        image_key = jnp.broadcast_to(lax.dynamic_index_in_dim(image_keys, kv_index, 0, keepdims=True), (2, image_rows, HEAD_SIZE))
        image_value = jnp.broadcast_to(lax.dynamic_index_in_dim(image_values, kv_index, 0, keepdims=True), (2, image_rows, HEAD_SIZE))
        cross_out = attend(query_one, image_key, image_value, everywhere)
        gate_factor = jnp.tanh(lax.dynamic_index_in_dim(cross_gate, head_index, 0, keepdims=False))
        return (self_out + gate_factor * cross_out).astype(jnp.bfloat16)
    per_head = lax.map(one_head, jnp.arange(HQ, dtype=jnp.int32))
    return jnp.transpose(per_head, (1, 2, 0, 3)).reshape(2, seq_len, HQ * HEAD_SIZE)
```

```python
import functools
import math

import jax
import jax.numpy as jnp
from jax import lax
from jax.experimental import pallas as pl
from jax.experimental.pallas import tpu as pltpu
from jax.sharding import PartitionSpec as P

HQ = 64
KVH = 8
HEAD_SIZE = 128


neg_large = -1e30


def fold_block(carry_state, query_grid, key_matrix, value_matrix, allowed, score_form, value_form):
    row_best, row_total, weighted = carry_state
    logit_scores = jnp.einsum(
        score_form, query_grid, key_matrix, preferred_element_type=jnp.float32
    ) * (1.0 / math.sqrt(HEAD_SIZE))
    masked = jnp.where(allowed, logit_scores, neg_large)
    new_best = jnp.maximum(row_best, jnp.max(masked, axis=-1))
    weights = jnp.where(allowed, jnp.exp(masked - new_best[..., None]), 0.0)
    shrink = jnp.exp(row_best - new_best)
    row_total = row_total * shrink + jnp.sum(weights, axis=-1)
    weighted = weighted * shrink[..., None] + jnp.einsum(
        value_form, weights.astype(jnp.bfloat16), value_matrix, preferred_element_type=jnp.float32
    )
    return (new_best, row_total, weighted)


def finish(carry_state):
    return jnp.transpose(carry_state[2] / carry_state[1][..., None], (0, 3, 1, 2, 4))


def scan_device(queries, self_kv, image_kv, cross_gate, lengths):
    tp_count = lax.axis_size("tp")
    heads_local = HQ // tp_count
    kv_local = max(1, KVH // tp_count)
    replicas = max(1, tp_count // KVH)
    heads_per_kv = heads_local // kv_local
    seq_rows = queries.shape[1]
    kv_cols = kv_local * 2 * HEAD_SIZE
    tp_rank = lax.axis_index("tp")
    own_pairs = lax.dynamic_slice_in_dim(self_kv, tp_rank // replicas * kv_cols, kv_cols, 2)
    query_grid = queries.reshape(2, seq_rows, kv_local, heads_per_kv, HEAD_SIZE)
    block_rank = lax.axis_index(("ctx", "section"))
    query_pos = block_rank * seq_rows + jnp.arange(seq_rows, dtype=jnp.int32)
    last_needed = jnp.minimum(block_rank * seq_rows + seq_rows - 1, jnp.max(lengths) - 1)
    start_state = (
        jnp.full((2, kv_local, heads_per_kv, seq_rows), neg_large, jnp.float32),
        jnp.zeros((2, kv_local, heads_per_kv, seq_rows), jnp.float32),
        jnp.zeros((2, kv_local, heads_per_kv, seq_rows, HEAD_SIZE), jnp.float32),
    )
    carry_state = start_state
    kv_piece = lax.all_gather(own_pairs, ("ctx", "section"), axis=1, tiled=True)
    row_count = kv_piece.shape[1]
    block_rows = math.gcd(row_count, 512)
    blocks = jnp.moveaxis(
        kv_piece.reshape(2, row_count // block_rows, block_rows, kv_local, 2, HEAD_SIZE), 1, 0
    )

    def self_one_block(inner_state, scan_item):
        block_number, block_pairs = scan_item
        block_first = block_number * block_rows
        key_pos = block_first + jnp.arange(block_rows, dtype=jnp.int32)
        allowed = (key_pos[None, None, :] <= query_pos[None, :, None]) & (
            key_pos[None, None, :] < lengths[:, None, None]
        )

        def compute_block(state_in):
            return fold_block(
                state_in,
                query_grid,
                block_pairs[:, :, :, 0],
                block_pairs[:, :, :, 1],
                allowed[:, None, None],
                "bsgrd,bpgd->bgrsp",
                "bgrsp,bpgd->bgrsd",
            )

        def keep_state(state_in):
            return state_in

        return (lax.cond(block_first > last_needed, keep_state, compute_block, inner_state), None)

    carry_state, _ = lax.scan(
        self_one_block, carry_state, (jnp.arange(row_count // block_rows, dtype=jnp.int32), blocks)
    )
    image_rows = image_kv.shape[0]
    copies = jnp.repeat(image_kv.reshape(image_rows, KVH // kv_local, kv_cols), replicas, axis=1)
    image_own = lax.all_to_all(
        copies.reshape(image_rows, tp_count * kv_cols),
        "tp",
        split_axis=1,
        concat_axis=0,
        tiled=True,
    )
    image_carry_state = start_state
    kv_piece = lax.all_gather(image_own, ("ctx", "section"), axis=0, tiled=True)
    row_count = kv_piece.shape[0]
    image_block_rows = math.gcd(row_count, 512)
    blocks = kv_piece.reshape(
        row_count // image_block_rows, image_block_rows, kv_local, 2, HEAD_SIZE
    )
    everywhere = jnp.ones((), jnp.bool_)

    def image_one_block(inner_state, block_pairs):
        return (
            fold_block(
                inner_state,
                query_grid,
                block_pairs[:, :, 0],
                block_pairs[:, :, 1],
                everywhere,
                "bsgrd,pgd->bgrsp",
                "bgrsp,pgd->bgrsd",
            ),
            None,
        )

    image_carry_state, _ = lax.scan(image_one_block, image_carry_state, blocks)
    gate_factor = jnp.tanh(cross_gate).reshape(1, 1, kv_local, heads_per_kv, 1)
    attended = finish(carry_state) + gate_factor * finish(image_carry_state)
    return attended.reshape(2, seq_rows, heads_local * HEAD_SIZE).astype(jnp.bfloat16)


NEG=-1e30
C2=math.log2(math.e)/math.sqrt(HEAD_SIZE)

def nt(a,b): return lax.dot_general(a,b,(((1,),(1,)),((),())),preferred_element_type=jnp.float32)
def nn(a,b): return lax.dot_general(a,b,(((1,),(0,)),((),())),preferred_element_type=jnp.float32)

def full_kernel(nblk, heads, rows, chunk, meta, gate, *refs):
    q_ref=refs[0]; blocks=refs[1:1+nblk]; img_ref=refs[1+nblk]; out_ref=refs[2+nblk]
    b=pl.program_id(0); g=pl.program_id(1)
    limit=meta[nblk+b]
    ki=lax.broadcasted_iota(jnp.int32,(1,rows),1)
    bias=[jnp.where(meta[i]+ki<limit,0.0,NEG) for i in range(nblk)]
    tri=lax.broadcasted_iota(jnp.int32,(rows,rows),1)<=lax.broadcasted_iota(jnp.int32,(rows,rows),0)
    own_bias=jnp.where(tri,bias[0],NEG)
    keys=jnp.concatenate([r[0,:,:HEAD_SIZE] for r in blocks],0)
    ones=jnp.ones((rows*nblk,HEAD_SIZE),jnp.bfloat16)
    vals=jnp.concatenate([jnp.concatenate([r[0,:,HEAD_SIZE:] for r in blocks],0),ones],1)
    n_img=img_ref.shape[0]
    ik=img_ref[:,:HEAD_SIZE]; iv=jnp.concatenate([img_ref[:,HEAD_SIZE:],jnp.ones((n_img,HEAD_SIZE),jnp.bfloat16)],1)
    for h0 in range(0,heads,chunk):
        qs=jnp.concatenate([q_ref[0,:,(h0+j)*HEAD_SIZE:(h0+j+1)*HEAD_SIZE] for j in range(chunk)],0)
        s=nt(qs,keys)
        si=nt(qs,ik)
        cols=[]
        for i in range(nblk):
            si_=s[:,i*rows:(i+1)*rows]
            if i==0: cols.append((si_.reshape(chunk,rows,rows)+own_bias[None]).reshape(chunk*rows,rows))
            else: cols.append(si_+bias[i])
        m=functools.reduce(jnp.maximum,cols)
        m=jnp.max(m,axis=1,keepdims=True)
        p=jnp.concatenate([jnp.exp2((c-m)*C2).astype(jnp.bfloat16) for c in cols],1)
        o=nn(p,vals)
        pi=jnp.exp2((si-jnp.max(si,axis=1,keepdims=True))*C2).astype(jnp.bfloat16)
        oi=nn(pi,iv)
        so=o[:,:HEAD_SIZE]/o[:,HEAD_SIZE:]
        co=oi[:,:HEAD_SIZE]/oi[:,HEAD_SIZE:]
        for j in range(chunk):
            gf=jnp.tanh(jnp.full((1,HEAD_SIZE),gate[g*heads+h0+j],jnp.float32))
            out_ref[0,:,(h0+j)*HEAD_SIZE:(h0+j+1)*HEAD_SIZE]=(so[j*rows:(j+1)*rows]+gf*co[j*rows:(j+1)*rows]).astype(jnp.bfloat16)

def attend_all(meta, gate, q, blocks, img, chunk=2):
    nb,rows,qc=q.shape
    kvl=blocks[0].shape[2]//(2*HEAD_SIZE)
    heads=qc//HEAD_SIZE//kvl
    nblk=len(blocks)
    blk=pl.BlockSpec((1,rows,2*HEAD_SIZE),lambda b,g,m,t: (b,0,g))
    qspec=pl.BlockSpec((1,rows,heads*HEAD_SIZE),lambda b,g,m,t:(b,0,g))
    grid_spec=pltpu.PrefetchScalarGridSpec(num_scalar_prefetch=2,grid=(nb,kvl),
        in_specs=[qspec]+[blk]*nblk+[pl.BlockSpec((img.shape[0],2*HEAD_SIZE),lambda b,g,m,t:(0,m[nblk+nb]*kvl+g))],
        out_specs=qspec)
    return pl.pallas_call(functools.partial(full_kernel,nblk,heads,rows,chunk),grid_spec=grid_spec,
        out_shape=jax.ShapeDtypeStruct(q.shape,jnp.bfloat16),
        compiler_params=pltpu.CompilerParams(vmem_limit_bytes=48<<20,dimension_semantics=("arbitrary","arbitrary")),
        name="attend")(meta,gate,q,*blocks,img)

def section_shift(block, step):
    count = lax.axis_size("section")
    return lax.ppermute(block, "section", [(z, (z + step) % count) for z in range(count)])


def ctx_swap(block):
    return lax.ppermute(block, "ctx", [(0, 1), (1, 0)])


def after(block, *others):
    return lax.optimization_barrier((block,) + others)[0]


def gather_rows(rows):
    for name in ("ctx", "section", "tp"):
        count = lax.axis_size(name)
        step = 1
        while step < count:
            other = lax.ppermute(rows, name, [(i, i ^ step) for i in range(count)])
            rows = jnp.concatenate([rows, other], 0)
            step *= 2
    return rows


def ring_device(queries, self_kv, image_kv, cross_gate, lengths):
    tp_count = lax.axis_size("tp")
    kv_local = KVH // tp_count
    seq_rows = queries.shape[1]
    kv_cols = kv_local * 2 * HEAD_SIZE
    tp_rank = lax.axis_index("tp")
    ctx = lax.axis_index("ctx")
    section = lax.axis_index("section")
    own = lax.dynamic_slice_in_dim(self_kv, tp_rank * kv_cols, kv_cols, 2)
    image = gather_rows(image_kv)
    r1 = section_shift(own, 1)
    y0 = ctx_swap(own)
    r3 = section_shift(after(own, r1), 3)
    y1 = ctx_swap(after(r1, y0))
    r2 = section_shift(after(r1, r3), 1)
    y3 = ctx_swap(after(r3, y1))
    y2 = ctx_swap(after(r2, y3))
    never = jnp.int32(1 << 30)
    firsts = [(ctx * 4 + section) * seq_rows]
    for k in (1, 2, 3):
        firsts.append(jnp.where(section >= k, (ctx * 4 + section - k) * seq_rows, never))
    for k in (0, 1, 2, 3):
        firsts.append(jnp.where(ctx == 1, (section - k) % 4 * seq_rows, never))
    meta = jnp.concatenate([jnp.stack(firsts), lengths, tp_rank[None]]).astype(jnp.int32)
    return attend_all(meta, cross_gate, queries, [own, r1, r2, r3, y0, y1, y2, y3], image, chunk=4)


def solution(mesh):
    placed = (
        P(None, ("ctx", "section"), "tp"),
        P(None, ("ctx", "section"), None),
        P(("ctx", "tp", "section"), None),
        P("tp"),
        P(),
    )
    few = mesh.shape["ctx"] == 2 and mesh.shape["section"] == 4 and mesh.shape["tp"] == 4
    return jax.shard_map(
        ring_device if few else scan_device,
        mesh=mesh,
        in_specs=placed,
        out_specs=P(None, ("ctx", "section"), "tp"),
        check_vma=False,
    )
```

```python
import functools
import math

import jax
import jax.numpy as jnp
from jax import lax
from jax.experimental import pallas as pl
from jax.experimental.pallas import tpu as pltpu
from jax.sharding import PartitionSpec as P

HQ = 64
KVH = 8
HEAD_SIZE = 128


neg_large = -1e30


def fold_block(carry_state, query_grid, key_matrix, value_matrix, allowed, score_form, value_form):
    row_best, row_total, weighted = carry_state
    logit_scores = jnp.einsum(
        score_form, query_grid, key_matrix, preferred_element_type=jnp.float32
    ) * (1.0 / math.sqrt(HEAD_SIZE))
    masked = jnp.where(allowed, logit_scores, neg_large)
    new_best = jnp.maximum(row_best, jnp.max(masked, axis=-1))
    weights = jnp.where(allowed, jnp.exp(masked - new_best[..., None]), 0.0)
    shrink = jnp.exp(row_best - new_best)
    row_total = row_total * shrink + jnp.sum(weights, axis=-1)
    weighted = weighted * shrink[..., None] + jnp.einsum(
        value_form, weights.astype(jnp.bfloat16), value_matrix, preferred_element_type=jnp.float32
    )
    return (new_best, row_total, weighted)


def finish(carry_state):
    return jnp.transpose(carry_state[2] / carry_state[1][..., None], (0, 3, 1, 2, 4))


def scan_device(queries, self_kv, image_kv, cross_gate, lengths):
    tp_count = lax.axis_size("tp")
    heads_local = HQ // tp_count
    kv_local = max(1, KVH // tp_count)
    replicas = max(1, tp_count // KVH)
    heads_per_kv = heads_local // kv_local
    seq_rows = queries.shape[1]
    kv_cols = kv_local * 2 * HEAD_SIZE
    tp_rank = lax.axis_index("tp")
    own_pairs = lax.dynamic_slice_in_dim(self_kv, tp_rank // replicas * kv_cols, kv_cols, 2)
    query_grid = queries.reshape(2, seq_rows, kv_local, heads_per_kv, HEAD_SIZE)
    block_rank = lax.axis_index(("ctx", "section"))
    query_pos = block_rank * seq_rows + jnp.arange(seq_rows, dtype=jnp.int32)
    last_needed = jnp.minimum(block_rank * seq_rows + seq_rows - 1, jnp.max(lengths) - 1)
    start_state = (
        jnp.full((2, kv_local, heads_per_kv, seq_rows), neg_large, jnp.float32),
        jnp.zeros((2, kv_local, heads_per_kv, seq_rows), jnp.float32),
        jnp.zeros((2, kv_local, heads_per_kv, seq_rows, HEAD_SIZE), jnp.float32),
    )
    carry_state = start_state
    kv_piece = lax.all_gather(own_pairs, ("ctx", "section"), axis=1, tiled=True)
    row_count = kv_piece.shape[1]
    block_rows = math.gcd(row_count, 512)
    blocks = jnp.moveaxis(
        kv_piece.reshape(2, row_count // block_rows, block_rows, kv_local, 2, HEAD_SIZE), 1, 0
    )

    def self_one_block(inner_state, scan_item):
        block_number, block_pairs = scan_item
        block_first = block_number * block_rows
        key_pos = block_first + jnp.arange(block_rows, dtype=jnp.int32)
        allowed = (key_pos[None, None, :] <= query_pos[None, :, None]) & (
            key_pos[None, None, :] < lengths[:, None, None]
        )

        def compute_block(state_in):
            return fold_block(
                state_in,
                query_grid,
                block_pairs[:, :, :, 0],
                block_pairs[:, :, :, 1],
                allowed[:, None, None],
                "bsgrd,bpgd->bgrsp",
                "bgrsp,bpgd->bgrsd",
            )

        def keep_state(state_in):
            return state_in

        return (lax.cond(block_first > last_needed, keep_state, compute_block, inner_state), None)

    carry_state, _ = lax.scan(
        self_one_block, carry_state, (jnp.arange(row_count // block_rows, dtype=jnp.int32), blocks)
    )
    image_rows = image_kv.shape[0]
    copies = jnp.repeat(image_kv.reshape(image_rows, KVH // kv_local, kv_cols), replicas, axis=1)
    image_own = lax.all_to_all(
        copies.reshape(image_rows, tp_count * kv_cols),
        "tp",
        split_axis=1,
        concat_axis=0,
        tiled=True,
    )
    image_carry_state = start_state
    kv_piece = lax.all_gather(image_own, ("ctx", "section"), axis=0, tiled=True)
    row_count = kv_piece.shape[0]
    image_block_rows = math.gcd(row_count, 512)
    blocks = kv_piece.reshape(
        row_count // image_block_rows, image_block_rows, kv_local, 2, HEAD_SIZE
    )
    everywhere = jnp.ones((), jnp.bool_)

    def image_one_block(inner_state, block_pairs):
        return (
            fold_block(
                inner_state,
                query_grid,
                block_pairs[:, :, 0],
                block_pairs[:, :, 1],
                everywhere,
                "bsgrd,pgd->bgrsp",
                "bgrsp,pgd->bgrsd",
            ),
            None,
        )

    image_carry_state, _ = lax.scan(image_one_block, image_carry_state, blocks)
    gate_factor = jnp.tanh(cross_gate).reshape(1, 1, kv_local, heads_per_kv, 1)
    attended = finish(carry_state) + gate_factor * finish(image_carry_state)
    return attended.reshape(2, seq_rows, heads_local * HEAD_SIZE).astype(jnp.bfloat16)


MASKED = -1e30
EXP2_SCALE = math.log2(math.e) / math.sqrt(HEAD_SIZE)
VMEM_SPEC = pl.BlockSpec(memory_space=pltpu.VMEM)
ANY_SPEC = pl.BlockSpec(memory_space=pl.ANY)
BLOCKS = 8
CHUNK = 4
KERNEL = pltpu.CompilerParams(vmem_limit_bytes=12 << 20)


def in_vmem(*arrays):
    return [pltpu.with_memory_space_constraint(array, pltpu.VMEM) for array in arrays]


def rows_by_rows(left, right):
    return lax.dot_general(left, right, (((1,), (1,)), ((), ())), preferred_element_type=jnp.float32)


def columns_by_columns(left, right):
    return lax.dot_general(left, right, (((0,), (0,)), ((), ())), preferred_element_type=jnp.float32)


def block_of(place):
    return jnp.where(place < BLOCKS // 2, place, 3 * BLOCKS // 2 - 1 - place)


def ring_blocks(shifts):
    ctx, section = lax.axis_index("ctx"), lax.axis_index("section")
    place = jnp.where(ctx == 0, section, BLOCKS - 1 - section)
    return [block_of((place + shift + BLOCKS) & (BLOCKS - 1)) for shift in shifts], ctx * (BLOCKS // 2) + section


def position_bias(block, own, limit, rows, diagonal):
    key = lax.broadcasted_iota(jnp.int32, (rows, rows), 0)
    first = jnp.where(block <= own, block * rows, 1 << 30)
    allowed = first + key < limit
    if diagonal:
        allowed &= key <= lax.broadcasted_iota(jnp.int32, (rows, rows), 1)
    return jnp.where(allowed, 0.0, MASKED)


def weigh(scores, biases, rows, old):
    if biases:
        scores = jnp.concatenate([scores[i * rows : (i + 1) * rows] + bias for i, bias in enumerate(biases)], 0)
    best = jnp.max(scores, axis=0, keepdims=True)
    if old is not None:
        best = jnp.maximum(old, best)
    weights = jnp.exp2((scores - best) * EXP2_SCALE)
    return best, jnp.sum(weights, axis=0, keepdims=True), weights.astype(jnp.bfloat16)


def weigh_heads(scores, biases, rows, heads, old):
    parts = []
    for h in range(heads):
        part = slice(h * rows, (h + 1) * rows)
        parts.append(weigh(scores[:, part], biases, rows, None if old is None else old[:, part]))
    return [jnp.concatenate(x, 1) for x in zip(*parts)]


def in_turn(units, score, weigh_unit, collect):
    ahead = score(*units[0])
    waiting = None
    for i, unit in enumerate(units):
        scores = ahead
        if i + 1 < len(units):
            ahead = score(*units[i + 1])
        weighed = weigh_unit(*unit, scores)
        if waiting is not None:
            collect(*waiting)
        waiting = (*unit, *weighed)
    collect(*waiting)


class Heads:
    def __init__(self, q_ref, groups):
        self.q_ref = q_ref
        self.sequences, self.rows = q_ref.shape[:2]
        self.heads = q_ref.shape[2] // HEAD_SIZE // groups
        self.chunk = min(CHUNK, self.heads)
        self.units = [
            (sequence, group, h)
            for group in range(groups)
            for sequence in range(self.sequences)
            for h in range(0, self.heads, self.chunk)
        ]

    def queries(self, sequence, group, h):
        first = (group * self.heads + h) * HEAD_SIZE
        columns = [slice(first + j * HEAD_SIZE, first + (j + 1) * HEAD_SIZE) for j in range(self.chunk)]
        return jnp.concatenate([self.q_ref[sequence, :, c] for c in columns], 0)

    def part(self, h):
        return slice(h * self.rows, (h + self.chunk) * self.rows)


def key_columns(group):
    return slice(2 * group * HEAD_SIZE, (2 * group + 1) * HEAD_SIZE)


def value_columns(group):
    return slice((2 * group + 1) * HEAD_SIZE, (2 * group + 2) * HEAD_SIZE)


def stack_rows(refs, sequence, columns):
    rows = [r[sequence if r.shape[0] > 1 else 0, :, columns] for r in refs]
    return jnp.concatenate(rows, 0) if len(rows) > 1 else rows[0]


def fold(heads, length_ref, blocks, numbers, own, old_state, state):
    stat_ref, sum_ref = state
    rows = heads.rows
    biases = [
        [
            position_bias(number, own, length_ref[i : i + 1], rows, old_state is None and j == 0)
            for j, number in enumerate(numbers)
        ]
        for i in range(heads.sequences)
    ]

    def score(sequence, group, h):
        return rows_by_rows(stack_rows(blocks, sequence, key_columns(group)), heads.queries(sequence, group, h))

    def weigh_unit(sequence, group, h, scores):
        part = heads.part(h)
        old = None if old_state is None else stat_ref[sequence, group, 0:1, part]
        best, total, weights = weigh_heads(scores, biases[sequence], rows, heads.chunk, old)
        shrink = None
        if old is not None:
            shrink = jnp.exp2((old - best) * EXP2_SCALE)
            total = stat_ref[sequence, group, 1:2, part] * shrink + total
        stat_ref[sequence, group, 0:1, part] = best
        stat_ref[sequence, group, 1:2, part] = total
        return shrink, weights

    def collect(sequence, group, h, shrink, weights):
        part = heads.part(h)
        added = columns_by_columns(stack_rows(blocks, sequence, value_columns(group)), weights)
        if shrink is not None:
            added = sum_ref[sequence, group, :, part] * shrink + added
        sum_ref[sequence, group, :, part] = added

    in_turn(heads.units, score, weigh_unit, collect)


def fold_kernel(first, shifts, groups, length_ref, q_ref, *refs):
    blocks = refs[: len(shifts)]
    numbers, own = ring_blocks(shifts)
    heads = Heads(q_ref, groups)
    if first:
        fold(heads, length_ref, blocks, numbers, own, None, refs[-2:])
    else:
        useful = functools.reduce(jnp.logical_or, [number < own for number in numbers])
        pl.when(useful)(lambda: fold(heads, length_ref, blocks, numbers, own, refs[-4:-2], refs[-2:]))


def state_shapes(q, groups):
    sequences, rows, columns = q.shape
    width = columns // HEAD_SIZE // groups * rows
    return [
        pltpu.VMEM((sequences, groups, 2, width), jnp.float32),
        pltpu.VMEM((sequences, groups, HEAD_SIZE, width), jnp.float32),
    ]


def cost(q, keys):
    work = q.shape[0] * q.shape[2] // HEAD_SIZE * q.shape[1] * keys
    return pl.CostEstimate(flops=work * 4 * HEAD_SIZE, bytes_accessed=1 << 20, transcendentals=work)


def fold_blocks(lengths, q, blocks, shifts, state):
    groups = blocks[0].shape[2] // (2 * HEAD_SIZE)
    first = state is None
    state = () if first else tuple(state)
    held = 2 + len(blocks)
    return pl.pallas_call(
        functools.partial(fold_kernel, first, shifts, groups),
        in_specs=[VMEM_SPEC] * (held + len(state)),
        out_specs=[VMEM_SPEC] * 2,
        out_shape=state_shapes(q, groups),
        input_output_aliases={} if first else {held + i: i for i in range(2)},
        compiler_params=KERNEL,
        cost_estimate=cost(q, q.shape[1] * len(blocks)),
        name="fold_blocks",
    )(*in_vmem(lengths, q, *blocks, *state))


def cross_kernel(groups, factor_ref, q_ref, *refs):
    images, cross_ref = refs[:-1], refs[-1]
    heads = Heads(q_ref, groups)
    rows = heads.rows
    first = lax.axis_index("tp") * 2 * groups
    columns = [pl.ds(pl.multiple_of((first + i) * HEAD_SIZE, HEAD_SIZE), HEAD_SIZE) for i in range(2 * groups)]
    image = [jnp.concatenate([r[:, c] for r in images], 0) for c in columns]

    def score(sequence, group, h):
        return rows_by_rows(image[2 * group], heads.queries(sequence, group, h))

    def weigh_unit(sequence, group, h, scores):
        _, total, weights = weigh_heads(scores, [], rows, heads.chunk, None)
        first = group * heads.heads + h
        factors = jnp.concatenate([factor_ref[first + j : first + j + 1] for j in range(heads.chunk)], 1)
        return factors / total, weights

    def collect(sequence, group, h, factors, weights):
        cross_ref[sequence, group, :, heads.part(h)] = columns_by_columns(image[2 * group + 1], weights) * factors

    in_turn(heads.units, score, weigh_unit, collect)


def cross_attend(factors, q, images, groups):
    return pl.pallas_call(
        functools.partial(cross_kernel, groups),
        in_specs=[VMEM_SPEC] * (2 + len(images)),
        out_specs=VMEM_SPEC,
        out_shape=state_shapes(q, groups)[1],
        compiler_params=KERNEL,
        cost_estimate=cost(q, q.shape[1]),
        name="cross_attend",
    )(*in_vmem(factors, q, *images))


def finish_kernel(shift, groups, length_ref, q_ref, block0, block1, cross_ref, stat_ref, sum_ref, out_ref):
    heads = Heads(q_ref, groups)
    rows = heads.rows
    (number,), own = ring_blocks([shift])
    blocks = (block0, block1)
    biases = [[position_bias(number, own, length_ref[i : i + 1], rows, False)] for i in range(heads.sequences)]

    def score(sequence, group, h):
        return rows_by_rows(blocks[sequence][0, :, key_columns(group)], heads.queries(sequence, group, h))

    def weigh_unit(sequence, group, h, scores):
        part = heads.part(h)
        old = stat_ref[sequence, group, 0:1, part]
        best, total, weights = weigh_heads(scores, biases[sequence], rows, heads.chunk, old)
        shrink = jnp.exp2((old - best) * EXP2_SCALE)
        over = 1.0 / (stat_ref[sequence, group, 1:2, part] * shrink + total)
        return shrink * over, over, weights

    def collect(sequence, group, h, old_factor, factor, weights):
        part = heads.part(h)
        added = columns_by_columns(blocks[sequence][0, :, value_columns(group)], weights)
        out = sum_ref[sequence, group, :, part] * old_factor + added * factor + cross_ref[sequence, group, :, part]
        for j in range(heads.chunk):
            first = (group * heads.heads + h + j) * HEAD_SIZE
            out_ref[sequence, :, first : first + HEAD_SIZE] = out[:, j * rows : (j + 1) * rows].T.astype(jnp.bfloat16)

    in_turn(heads.units, score, weigh_unit, collect)


def finish_rows(lengths, q, shift, blocks, cross, state):
    groups = blocks[0].shape[2] // (2 * HEAD_SIZE)
    args = in_vmem(lengths, q, *blocks, cross, *state)
    return pl.pallas_call(
        functools.partial(finish_kernel, shift, groups),
        in_specs=[VMEM_SPEC] * len(args),
        out_specs=VMEM_SPEC,
        out_shape=jax.ShapeDtypeStruct(q.shape, q.dtype),
        compiler_params=KERNEL,
        cost_estimate=cost(q, q.shape[1]),
        name="finish_rows",
    )(*args)


def load_kernel(lengths, gate, q_ref, image_ref, limit_ref, factor_ref, q_out, image_out, counts, gates, sems):
    pairs = ((lengths, counts), (gate, gates), (q_ref, q_out), (image_ref, image_out))
    copies = [pltpu.make_async_copy(source, target, sems.at[i]) for i, (source, target) in enumerate(pairs)]
    for copy in copies:
        copy.start()
    copies[0].wait()
    for i in range(limit_ref.shape[0]):
        limit_ref[i : i + 1] = jnp.full((1, limit_ref.shape[1]), counts[i], jnp.int32)
    copies[1].wait()
    for i in range(factor_ref.shape[0]):
        factor_ref[i : i + 1] = jnp.full((1, factor_ref.shape[1]), gates[i], jnp.float32)
    factor_ref[...] = jnp.tanh(factor_ref[...])
    copies[2].wait()
    copies[3].wait()


def load_inputs(*arrays):
    lengths, gate, q, image = arrays
    rows = q.shape[1]
    return pl.pallas_call(
        load_kernel,
        in_specs=[ANY_SPEC] * 4,
        out_specs=[VMEM_SPEC] * 4,
        out_shape=[
            pltpu.VMEM((lengths.shape[0], rows), jnp.int32),
            pltpu.VMEM((gate.shape[0], rows), jnp.float32),
            pltpu.VMEM(q.shape, q.dtype),
            pltpu.VMEM(image.shape, image.dtype),
        ],
        scratch_shapes=[
            pltpu.SMEM(lengths.shape, lengths.dtype),
            pltpu.SMEM(gate.shape, gate.dtype),
            pltpu.SemaphoreType.DMA((4,)),
        ],
        compiler_params=KERNEL,
        name="load_inputs",
    )(*[pltpu.with_memory_space_constraint(array, pltpu.HBM) for array in arrays])


def halve_kernel(forward_ref, backward_ref, first_ref, second_ref):
    first_ref[...] = forward_ref[0:1]
    second_ref[...] = backward_ref[1:2]


def half_of_each(forward, backward):
    shape = pltpu.VMEM((1,) + forward.shape[1:], forward.dtype)
    return pl.pallas_call(
        halve_kernel,
        in_specs=[VMEM_SPEC] * 2,
        out_specs=[VMEM_SPEC] * 2,
        out_shape=[shape] * 2,
        compiler_params=KERNEL,
        name="half_of_each",
    )(*in_vmem(forward, backward))


RING = (0, 1, 2, 3, 7, 6, 5, 4)


def ring_forward(block):
    pairs = [(RING[i], RING[(i + 1) % BLOCKS]) for i in range(BLOCKS)]
    return lax.ppermute(block, ("ctx", "section"), pairs)


def ring_backward(block):
    pairs = [(RING[(i + 1) % BLOCKS], RING[i]) for i in range(BLOCKS)]
    return lax.ppermute(block, ("ctx", "section"), pairs)


def after(block, *others):
    return lax.optimization_barrier((block,) + others)[0]


def swapped(rows, name, bits):
    return lax.ppermute(rows, name, [(i, i ^ bits) for i in range(lax.axis_size(name))])


def ring_device(queries, self_kv, image_kv, cross_gate, lengths):
    tp_count = lax.axis_size("tp")
    groups = KVH // tp_count
    kv_cols = groups * 2 * HEAD_SIZE
    own = lax.dynamic_slice_in_dim(self_kv, lax.axis_index("tp") * kv_cols, kv_cols, 2)
    f1, b1 = ring_forward(own), ring_backward(own)
    i1 = swapped(image_kv, "section", 2)
    limits, factors, q, image1 = load_inputs(lengths, cross_gate, queries, image_kv)
    image2 = jnp.concatenate([image1, i1], 0)
    i2 = swapped(image2, "section", 1)

    f2, b2 = ring_forward(after(f1, image2)), ring_backward(after(b1, image2))
    image4 = jnp.concatenate([image2, i2], 0)
    i3 = swapped(image4, "ctx", 1)
    state = fold_blocks(limits, q, [own, f1, after(b1, image4)], (0, -1, 1), None)

    f3, b3 = ring_forward(after(f2, state[0])), ring_backward(after(b2, state[0]))
    image8 = jnp.concatenate([image4, i3], 0)
    images = [image8] + [swapped(image8, "tp", bits) for bits in range(1, tp_count)]
    state = fold_blocks(limits, q, [f2, after(b2, image8)], (-2, 2), state)

    f4, b4 = half_of_each(after(f3, state[0], *images), b3)
    f4, b4 = ring_forward(f4), ring_backward(b4)
    cross = cross_attend(factors, q, images, groups)
    state = fold_blocks(limits, q, [f3, b3], (-3, 3), state)
    return finish_rows(limits, q, 4, [f4, b4], cross, state)


def solution(mesh):
    placed = (
        P(None, ("ctx", "section"), "tp"),
        P(None, ("ctx", "section"), None),
        P(("ctx", "tp", "section"), None),
        P("tp"),
        P(),
    )
    ring = mesh.shape["ctx"] == 2 and mesh.shape["section"] == 4 and mesh.shape["tp"] == 4
    return jax.shard_map(
        ring_device if ring else scan_device,
        mesh=mesh,
        in_specs=placed,
        out_specs=P(None, ("ctx", "section"), "tp"),
        check_vma=False,
    )
```

```python
import functools
import math

import jax
import jax.numpy as jnp
from jax import lax
from jax.experimental import pallas as pl
from jax.experimental.pallas import tpu as pltpu
from jax.sharding import PartitionSpec as P

HQ = 64
KVH = 8
HEAD_SIZE = 128


neg_large = -1e30


def fold_block(carry_state, query_grid, key_matrix, value_matrix, allowed, score_form, value_form):
    row_best, row_total, weighted = carry_state
    logit_scores = jnp.einsum(
        score_form, query_grid, key_matrix, preferred_element_type=jnp.float32
    ) * (1.0 / math.sqrt(HEAD_SIZE))
    masked = jnp.where(allowed, logit_scores, neg_large)
    new_best = jnp.maximum(row_best, jnp.max(masked, axis=-1))
    weights = jnp.where(allowed, jnp.exp(masked - new_best[..., None]), 0.0)
    shrink = jnp.exp(row_best - new_best)
    row_total = row_total * shrink + jnp.sum(weights, axis=-1)
    weighted = weighted * shrink[..., None] + jnp.einsum(
        value_form, weights.astype(jnp.bfloat16), value_matrix, preferred_element_type=jnp.float32
    )
    return (new_best, row_total, weighted)


def finish(carry_state):
    return jnp.transpose(carry_state[2] / carry_state[1][..., None], (0, 3, 1, 2, 4))


def scan_device(queries, self_kv, image_kv, cross_gate, lengths):
    tp_count = lax.axis_size("tp")
    heads_local = HQ // tp_count
    kv_local = max(1, KVH // tp_count)
    replicas = max(1, tp_count // KVH)
    heads_per_kv = heads_local // kv_local
    seq_rows = queries.shape[1]
    kv_cols = kv_local * 2 * HEAD_SIZE
    tp_rank = lax.axis_index("tp")
    own_pairs = lax.dynamic_slice_in_dim(self_kv, tp_rank // replicas * kv_cols, kv_cols, 2)
    query_grid = queries.reshape(2, seq_rows, kv_local, heads_per_kv, HEAD_SIZE)
    block_rank = lax.axis_index(("ctx", "section"))
    query_pos = block_rank * seq_rows + jnp.arange(seq_rows, dtype=jnp.int32)
    last_needed = jnp.minimum(block_rank * seq_rows + seq_rows - 1, jnp.max(lengths) - 1)
    start_state = (
        jnp.full((2, kv_local, heads_per_kv, seq_rows), neg_large, jnp.float32),
        jnp.zeros((2, kv_local, heads_per_kv, seq_rows), jnp.float32),
        jnp.zeros((2, kv_local, heads_per_kv, seq_rows, HEAD_SIZE), jnp.float32),
    )
    carry_state = start_state
    kv_piece = lax.all_gather(own_pairs, ("ctx", "section"), axis=1, tiled=True)
    row_count = kv_piece.shape[1]
    block_rows = math.gcd(row_count, 512)
    blocks = jnp.moveaxis(
        kv_piece.reshape(2, row_count // block_rows, block_rows, kv_local, 2, HEAD_SIZE), 1, 0
    )

    def self_one_block(inner_state, scan_item):
        block_number, block_pairs = scan_item
        block_first = block_number * block_rows
        key_pos = block_first + jnp.arange(block_rows, dtype=jnp.int32)
        allowed = (key_pos[None, None, :] <= query_pos[None, :, None]) & (
            key_pos[None, None, :] < lengths[:, None, None]
        )

        def compute_block(state_in):
            return fold_block(
                state_in,
                query_grid,
                block_pairs[:, :, :, 0],
                block_pairs[:, :, :, 1],
                allowed[:, None, None],
                "bsgrd,bpgd->bgrsp",
                "bgrsp,bpgd->bgrsd",
            )

        def keep_state(state_in):
            return state_in

        return (lax.cond(block_first > last_needed, keep_state, compute_block, inner_state), None)

    carry_state, _ = lax.scan(
        self_one_block, carry_state, (jnp.arange(row_count // block_rows, dtype=jnp.int32), blocks)
    )
    image_rows = image_kv.shape[0]
    copies = jnp.repeat(image_kv.reshape(image_rows, KVH // kv_local, kv_cols), replicas, axis=1)
    image_own = lax.all_to_all(
        copies.reshape(image_rows, tp_count * kv_cols),
        "tp",
        split_axis=1,
        concat_axis=0,
        tiled=True,
    )
    image_carry_state = start_state
    kv_piece = lax.all_gather(image_own, ("ctx", "section"), axis=0, tiled=True)
    row_count = kv_piece.shape[0]
    image_block_rows = math.gcd(row_count, 512)
    blocks = kv_piece.reshape(
        row_count // image_block_rows, image_block_rows, kv_local, 2, HEAD_SIZE
    )
    everywhere = jnp.ones((), jnp.bool_)

    def image_one_block(inner_state, block_pairs):
        return (
            fold_block(
                inner_state,
                query_grid,
                block_pairs[:, :, 0],
                block_pairs[:, :, 1],
                everywhere,
                "bsgrd,pgd->bgrsp",
                "bgrsp,pgd->bgrsd",
            ),
            None,
        )

    image_carry_state, _ = lax.scan(image_one_block, image_carry_state, blocks)
    gate_factor = jnp.tanh(cross_gate).reshape(1, 1, kv_local, heads_per_kv, 1)
    attended = finish(carry_state) + gate_factor * finish(image_carry_state)
    return attended.reshape(2, seq_rows, heads_local * HEAD_SIZE).astype(jnp.bfloat16)


MASKED = -1e30
EXP2_SCALE = math.log2(math.e) / math.sqrt(HEAD_SIZE)
VMEM_SPEC = pl.BlockSpec(memory_space=pltpu.VMEM)
ANY_SPEC = pl.BlockSpec(memory_space=pl.ANY)
BLOCKS = 8
CHUNK = 4
KERNEL = pltpu.CompilerParams(vmem_limit_bytes=12 << 20)


def in_vmem(*arrays):
    return [pltpu.with_memory_space_constraint(array, pltpu.VMEM) for array in arrays]


def rows_by_rows(left, right):
    return lax.dot_general(left, right, (((1,), (1,)), ((), ())), preferred_element_type=jnp.float32)


def columns_by_columns(left, right):
    return lax.dot_general(left, right, (((0,), (0,)), ((), ())), preferred_element_type=jnp.float32)


def block_of(place):
    return jnp.where(place < BLOCKS // 2, place, 3 * BLOCKS // 2 - 1 - place)


def ring_blocks(shifts):
    ctx, section = lax.axis_index("ctx"), lax.axis_index("section")
    place = jnp.where(ctx == 0, section, BLOCKS - 1 - section)
    return [block_of((place + shift + BLOCKS) & (BLOCKS - 1)) for shift in shifts], ctx * (BLOCKS // 2) + section


def position_bias(block, own, limit, rows, diagonal):
    key = lax.broadcasted_iota(jnp.int32, (rows, rows), 0)
    first = jnp.where(block <= own, block * rows, 1 << 30)
    allowed = first + key < limit
    if diagonal:
        allowed &= key <= lax.broadcasted_iota(jnp.int32, (rows, rows), 1)
    return jnp.where(allowed, 0.0, MASKED)


def weigh(scores, biases, rows, old):
    if biases:
        scores = jnp.concatenate([scores[i * rows : (i + 1) * rows] + bias for i, bias in enumerate(biases)], 0)
    best = jnp.max(scores, axis=0, keepdims=True)
    if old is not None:
        best = jnp.maximum(old, best)
    weights = jnp.exp2((scores - best) * EXP2_SCALE)
    return best, jnp.sum(weights, axis=0, keepdims=True), weights.astype(jnp.bfloat16)


def weigh_heads(scores, biases, rows, heads, old):
    parts = []
    for h in range(heads):
        part = slice(h * rows, (h + 1) * rows)
        parts.append(weigh(scores[:, part], biases, rows, None if old is None else old[:, part]))
    return [jnp.concatenate(x, 1) for x in zip(*parts)]


def in_turn(units, score, weigh_unit, collect):
    ahead = score(*units[0])
    waiting = None
    for i, unit in enumerate(units):
        scores = ahead
        if i + 1 < len(units):
            ahead = score(*units[i + 1])
        weighed = weigh_unit(*unit, scores)
        if waiting is not None:
            collect(*waiting)
        waiting = (*unit, *weighed)
    collect(*waiting)


class Heads:
    def __init__(self, q_ref, groups):
        self.q_ref = q_ref
        self.sequences, self.rows = q_ref.shape[:2]
        self.heads = q_ref.shape[2] // HEAD_SIZE // groups
        self.chunk = min(CHUNK, self.heads)
        self.units = [
            (sequence, group, h)
            for group in range(groups)
            for sequence in range(self.sequences)
            for h in range(0, self.heads, self.chunk)
        ]

    def queries(self, sequence, group, h):
        first = (group * self.heads + h) * HEAD_SIZE
        columns = [slice(first + j * HEAD_SIZE, first + (j + 1) * HEAD_SIZE) for j in range(self.chunk)]
        return jnp.concatenate([self.q_ref[sequence, :, c] for c in columns], 0)

    def part(self, h):
        return slice(h * self.rows, (h + self.chunk) * self.rows)


def key_columns(group):
    return slice(2 * group * HEAD_SIZE, (2 * group + 1) * HEAD_SIZE)


def value_columns(group):
    return slice((2 * group + 1) * HEAD_SIZE, (2 * group + 2) * HEAD_SIZE)


def stack_rows(refs, sequence, columns):
    rows = [r[sequence if r.shape[0] > 1 else 0, :, columns] for r in refs]
    return jnp.concatenate(rows, 0) if len(rows) > 1 else rows[0]


def fold(heads, length_ref, blocks, numbers, own, old_state, state):
    stat_ref, sum_ref = state
    rows = heads.rows
    biases = [
        [
            position_bias(number, own, length_ref[i : i + 1], rows, old_state is None and j == 0)
            for j, number in enumerate(numbers)
        ]
        for i in range(heads.sequences)
    ]

    def score(sequence, group, h):
        return rows_by_rows(stack_rows(blocks, sequence, key_columns(group)), heads.queries(sequence, group, h))

    def weigh_unit(sequence, group, h, scores):
        part = heads.part(h)
        old = None if old_state is None else stat_ref[sequence, group, 0:1, part]
        best, total, weights = weigh_heads(scores, biases[sequence], rows, heads.chunk, old)
        shrink = None
        if old is not None:
            shrink = jnp.exp2((old - best) * EXP2_SCALE)
            total = stat_ref[sequence, group, 1:2, part] * shrink + total
        stat_ref[sequence, group, 0:1, part] = best
        stat_ref[sequence, group, 1:2, part] = total
        return shrink, weights

    def collect(sequence, group, h, shrink, weights):
        part = heads.part(h)
        added = columns_by_columns(stack_rows(blocks, sequence, value_columns(group)), weights)
        if shrink is not None:
            added = sum_ref[sequence, group, :, part] * shrink + added
        sum_ref[sequence, group, :, part] = added

    in_turn(heads.units, score, weigh_unit, collect)


def fold_kernel(first, shifts, groups, length_ref, q_ref, *refs):
    blocks = refs[: len(shifts)]
    numbers, own = ring_blocks(shifts)
    heads = Heads(q_ref, groups)
    if first:
        fold(heads, length_ref, blocks, numbers, own, None, refs[-2:])
    else:
        useful = functools.reduce(jnp.logical_or, [number < own for number in numbers])
        pl.when(useful)(lambda: fold(heads, length_ref, blocks, numbers, own, refs[-4:-2], refs[-2:]))


def state_shapes(q, groups):
    sequences, rows, columns = q.shape
    width = columns // HEAD_SIZE // groups * rows
    return [
        pltpu.VMEM((sequences, groups, 2, width), jnp.float32),
        pltpu.VMEM((sequences, groups, HEAD_SIZE, width), jnp.float32),
    ]


def cost(q, keys):
    work = q.shape[0] * q.shape[2] // HEAD_SIZE * q.shape[1] * keys
    return pl.CostEstimate(flops=work * 4 * HEAD_SIZE, bytes_accessed=1 << 20, transcendentals=work)


def fold_blocks(lengths, q, blocks, shifts, state):
    groups = blocks[0].shape[2] // (2 * HEAD_SIZE)
    first = state is None
    state = () if first else tuple(state)
    held = 2 + len(blocks)
    return pl.pallas_call(
        functools.partial(fold_kernel, first, shifts, groups),
        in_specs=[VMEM_SPEC] * (held + len(state)),
        out_specs=[VMEM_SPEC] * 2,
        out_shape=state_shapes(q, groups),
        input_output_aliases={} if first else {held + i: i for i in range(2)},
        compiler_params=KERNEL,
        cost_estimate=cost(q, q.shape[1] * len(blocks)),
        name="fold_blocks",
    )(*in_vmem(lengths, q, *blocks, *state))


def cross_kernel(groups, factor_ref, q_ref, *refs):
    images, cross_ref = refs[:-1], refs[-1]
    heads = Heads(q_ref, groups)
    rows = heads.rows
    first = lax.axis_index("tp") * 2 * groups
    columns = [pl.ds(pl.multiple_of((first + i) * HEAD_SIZE, HEAD_SIZE), HEAD_SIZE) for i in range(2 * groups)]
    image = [jnp.concatenate([r[:, c] for r in images], 0) for c in columns]

    def score(sequence, group, h):
        return rows_by_rows(image[2 * group], heads.queries(sequence, group, h))

    def weigh_unit(sequence, group, h, scores):
        _, total, weights = weigh_heads(scores, [], rows, heads.chunk, None)
        first = group * heads.heads + h
        factors = jnp.concatenate([factor_ref[first + j : first + j + 1] for j in range(heads.chunk)], 1)
        return factors / total, weights

    def collect(sequence, group, h, factors, weights):
        cross_ref[sequence, group, :, heads.part(h)] = columns_by_columns(image[2 * group + 1], weights) * factors

    in_turn(heads.units, score, weigh_unit, collect)


def cross_attend(factors, q, images, groups):
    return pl.pallas_call(
        functools.partial(cross_kernel, groups),
        in_specs=[VMEM_SPEC] * (2 + len(images)),
        out_specs=VMEM_SPEC,
        out_shape=state_shapes(q, groups)[1],
        compiler_params=KERNEL,
        cost_estimate=cost(q, q.shape[1]),
        name="cross_attend",
    )(*in_vmem(factors, q, *images))


class Results:
    def __init__(self, heads, out_ref, held_ref, sems):
        self.heads, self.out_ref, self.held_ref, self.sems = heads, out_ref, held_ref, sems
        self.copies = []

    def put(self, sequence, group, h, out):
        heads = self.heads
        rows = heads.rows
        for j in range(heads.chunk):
            first = (group * heads.heads + h + j) * HEAD_SIZE
            turned = out[:, j * rows : (j + 1) * rows].T.astype(jnp.bfloat16)
            self.held_ref[sequence, :, first : first + HEAD_SIZE] = turned
        if h + heads.chunk == heads.heads:
            width = heads.heads * HEAD_SIZE
            at = (sequence, slice(None), pl.ds(group * width, width))
            copy = pltpu.make_async_copy(self.held_ref.at[at], self.out_ref.at[at], self.sems.at[sequence, group])
            copy.start()
            self.copies.append(copy)

    def wait(self):
        for copy in self.copies:
            copy.wait()


def result_scratch(q, groups):
    return [pltpu.VMEM(q.shape, q.dtype), pltpu.SemaphoreType.DMA((q.shape[0], groups))]


def fold_or_finish_kernel(shifts, last_shift, groups, length_ref, q_ref, *refs):
    blocks = refs[: len(shifts)]
    cross_ref = refs[len(shifts)]
    out_ref, stat_ref, sum_ref, held_ref, sems = refs[-5:]
    numbers, own = ring_blocks(shifts)
    (last,), _ = ring_blocks([last_shift])
    heads = Heads(q_ref, groups)
    useful = functools.reduce(jnp.logical_or, [number < own for number in numbers])
    state = (stat_ref, sum_ref)
    pl.when(useful)(lambda: fold(heads, length_ref, blocks, numbers, own, state, state))

    def write():
        results = Results(heads, out_ref, held_ref, sems)
        for sequence, group, h in heads.units:
            part = heads.part(h)
            over = 1.0 / stat_ref[sequence, group, 1:2, part]
            results.put(
                sequence, group, h, sum_ref[sequence, group, :, part] * over + cross_ref[sequence, group, :, part]
            )
        results.wait()

    pl.when(last > own)(write)


def fold_or_finish(lengths, q, blocks, shifts, last_shift, cross, state):
    groups = blocks[0].shape[2] // (2 * HEAD_SIZE)
    args = in_vmem(lengths, q, *blocks, cross, *state)
    return pl.pallas_call(
        functools.partial(fold_or_finish_kernel, shifts, last_shift, groups),
        in_specs=[VMEM_SPEC] * len(args),
        out_specs=[ANY_SPEC] + [VMEM_SPEC] * 2,
        out_shape=[pltpu.HBM(q.shape, q.dtype)] + state_shapes(q, groups),
        scratch_shapes=result_scratch(q, groups),
        input_output_aliases={len(args) - 2: 1, len(args) - 1: 2},
        compiler_params=KERNEL,
        cost_estimate=cost(q, q.shape[1] * len(blocks)),
        name="fold_or_finish",
    )(*args)


def finish_kernel(shift, groups, length_ref, q_ref, block0, block1, cross_ref, stat_ref, sum_ref, _, out_ref, held_ref, sems):
    heads = Heads(q_ref, groups)
    rows = heads.rows
    (number,), own = ring_blocks([shift])
    blocks = (block0, block1)

    def work():
        biases = [[position_bias(number, own, length_ref[i : i + 1], rows, False)] for i in range(heads.sequences)]
        results = Results(heads, out_ref, held_ref, sems)

        def score(sequence, group, h):
            return rows_by_rows(blocks[sequence][0, :, key_columns(group)], heads.queries(sequence, group, h))

        def weigh_unit(sequence, group, h, scores):
            part = heads.part(h)
            old = stat_ref[sequence, group, 0:1, part]
            best, total, weights = weigh_heads(scores, biases[sequence], rows, heads.chunk, old)
            shrink = jnp.exp2((old - best) * EXP2_SCALE)
            over = 1.0 / (stat_ref[sequence, group, 1:2, part] * shrink + total)
            return shrink * over, over, weights

        def collect(sequence, group, h, old_factor, factor, weights):
            part = heads.part(h)
            added = columns_by_columns(blocks[sequence][0, :, value_columns(group)], weights)
            out = sum_ref[sequence, group, :, part] * old_factor + added * factor + cross_ref[sequence, group, :, part]
            results.put(sequence, group, h, out)

        in_turn(heads.units, score, weigh_unit, collect)
        results.wait()

    pl.when(number < own)(work)


def finish_rows(lengths, q, shift, blocks, cross, state, result):
    groups = blocks[0].shape[2] // (2 * HEAD_SIZE)
    args = in_vmem(lengths, q, *blocks, cross, *state)
    return pl.pallas_call(
        functools.partial(finish_kernel, shift, groups),
        in_specs=[VMEM_SPEC] * len(args) + [ANY_SPEC],
        out_specs=ANY_SPEC,
        out_shape=pltpu.HBM(q.shape, q.dtype),
        scratch_shapes=result_scratch(q, groups),
        input_output_aliases={len(args): 0},
        compiler_params=KERNEL,
        cost_estimate=cost(q, q.shape[1]),
        name="finish_rows",
    )(*args, result)


def load_kernel(lengths, gate, q_ref, image_ref, limit_ref, factor_ref, q_out, image_out, counts, gates, sems):
    pairs = ((lengths, counts), (gate, gates), (q_ref, q_out), (image_ref, image_out))
    copies = [pltpu.make_async_copy(source, target, sems.at[i]) for i, (source, target) in enumerate(pairs)]
    for copy in copies:
        copy.start()
    copies[0].wait()
    for i in range(limit_ref.shape[0]):
        limit_ref[i : i + 1] = jnp.full((1, limit_ref.shape[1]), counts[i], jnp.int32)
    copies[1].wait()
    for i in range(factor_ref.shape[0]):
        factor_ref[i : i + 1] = jnp.full((1, factor_ref.shape[1]), gates[i], jnp.float32)
    factor_ref[...] = jnp.tanh(factor_ref[...])
    copies[2].wait()
    copies[3].wait()


def load_inputs(*arrays):
    lengths, gate, q, image = arrays
    rows = q.shape[1]
    return pl.pallas_call(
        load_kernel,
        in_specs=[ANY_SPEC] * 4,
        out_specs=[VMEM_SPEC] * 4,
        out_shape=[
            pltpu.VMEM((lengths.shape[0], rows), jnp.int32),
            pltpu.VMEM((gate.shape[0], rows), jnp.float32),
            pltpu.VMEM(q.shape, q.dtype),
            pltpu.VMEM(image.shape, image.dtype),
        ],
        scratch_shapes=[
            pltpu.SMEM(lengths.shape, lengths.dtype),
            pltpu.SMEM(gate.shape, gate.dtype),
            pltpu.SemaphoreType.DMA((4,)),
        ],
        compiler_params=KERNEL,
        name="load_inputs",
    )(*[pltpu.with_memory_space_constraint(array, pltpu.HBM) for array in arrays])


def halve_kernel(forward_ref, backward_ref, first_ref, second_ref):
    first_ref[...] = forward_ref[0:1]
    second_ref[...] = backward_ref[1:2]


def half_of_each(forward, backward):
    shape = pltpu.VMEM((1,) + forward.shape[1:], forward.dtype)
    return pl.pallas_call(
        halve_kernel,
        in_specs=[VMEM_SPEC] * 2,
        out_specs=[VMEM_SPEC] * 2,
        out_shape=[shape] * 2,
        compiler_params=KERNEL,
        name="half_of_each",
    )(*in_vmem(forward, backward))


RING = (0, 1, 2, 3, 7, 6, 5, 4)


def ring_forward(block):
    pairs = [(RING[i], RING[(i + 1) % BLOCKS]) for i in range(BLOCKS)]
    return lax.ppermute(block, ("ctx", "section"), pairs)


def ring_backward(block):
    pairs = [(RING[(i + 1) % BLOCKS], RING[i]) for i in range(BLOCKS)]
    return lax.ppermute(block, ("ctx", "section"), pairs)


def after(block, *others):
    return lax.optimization_barrier((block,) + others)[0]


def swapped(rows, name, bits):
    return lax.ppermute(rows, name, [(i, i ^ bits) for i in range(lax.axis_size(name))])


def ring_device(queries, self_kv, image_kv, cross_gate, lengths):
    tp_count = lax.axis_size("tp")
    groups = KVH // tp_count
    kv_cols = groups * 2 * HEAD_SIZE
    own = lax.dynamic_slice_in_dim(self_kv, lax.axis_index("tp") * kv_cols, kv_cols, 2)
    f1, b1 = ring_forward(own), ring_backward(own)
    i1 = swapped(image_kv, "section", 2)
    limits, factors, q, image1 = load_inputs(lengths, cross_gate, queries, image_kv)
    image2 = jnp.concatenate([image1, i1], 0)
    i2 = swapped(image2, "section", 1)

    f2, b2 = ring_forward(after(f1, image2)), ring_backward(after(b1, image2))
    image4 = jnp.concatenate([image2, i2], 0)
    i3 = swapped(image4, "ctx", 1)
    state = fold_blocks(limits, q, [own, f1, after(b1, image4)], (0, -1, 1), None)

    f3, b3 = ring_forward(after(f2, state[0])), ring_backward(after(b2, state[0]))
    image8 = jnp.concatenate([image4, i3], 0)
    images = [image8] + [swapped(image8, "tp", bits) for bits in range(1, tp_count)]
    state = fold_blocks(limits, q, [f2, after(b2, image8)], (-2, 2), state)

    f4, b4 = half_of_each(after(f3, state[0], *images), b3)
    f4, b4 = ring_forward(f4), ring_backward(b4)
    cross = cross_attend(factors, q, images, groups)
    result, *state = fold_or_finish(limits, q, [f3, b3], (-3, 3), 4, cross, state)
    return finish_rows(limits, q, 4, [f4, b4], cross, state, result)


def solution(mesh):
    placed = (
        P(None, ("ctx", "section"), "tp"),
        P(None, ("ctx", "section"), None),
        P(("ctx", "tp", "section"), None),
        P("tp"),
        P(),
    )
    ring = mesh.shape["ctx"] == 2 and mesh.shape["section"] == 4 and mesh.shape["tp"] == 4
    return jax.shard_map(
        ring_device if ring else scan_device,
        mesh=mesh,
        in_specs=placed,
        out_specs=P(None, ("ctx", "section"), "tp"),
        check_vma=False,
    )
```

```python
import functools
import math

import jax
import jax.numpy as jnp
from jax import lax
from jax.experimental import pallas as pl
from jax.experimental.pallas import tpu as pltpu
from jax.sharding import PartitionSpec as P

HQ = 64
KVH = 8
HEAD_SIZE = 128


neg_large = -1e30


def fold_block(carry_state, query_grid, key_matrix, value_matrix, allowed, score_form, value_form):
    row_best, row_total, weighted = carry_state
    logit_scores = jnp.einsum(
        score_form, query_grid, key_matrix, preferred_element_type=jnp.float32
    ) * (1.0 / math.sqrt(HEAD_SIZE))
    masked = jnp.where(allowed, logit_scores, neg_large)
    new_best = jnp.maximum(row_best, jnp.max(masked, axis=-1))
    weights = jnp.where(allowed, jnp.exp(masked - new_best[..., None]), 0.0)
    shrink = jnp.exp(row_best - new_best)
    row_total = row_total * shrink + jnp.sum(weights, axis=-1)
    weighted = weighted * shrink[..., None] + jnp.einsum(
        value_form, weights.astype(jnp.bfloat16), value_matrix, preferred_element_type=jnp.float32
    )
    return (new_best, row_total, weighted)


def finish(carry_state):
    return jnp.transpose(carry_state[2] / carry_state[1][..., None], (0, 3, 1, 2, 4))


def scan_device(queries, self_kv, image_kv, cross_gate, lengths):
    tp_count = lax.axis_size("tp")
    heads_local = HQ // tp_count
    kv_local = max(1, KVH // tp_count)
    replicas = max(1, tp_count // KVH)
    heads_per_kv = heads_local // kv_local
    seq_rows = queries.shape[1]
    kv_cols = kv_local * 2 * HEAD_SIZE
    tp_rank = lax.axis_index("tp")
    own_pairs = lax.dynamic_slice_in_dim(self_kv, tp_rank // replicas * kv_cols, kv_cols, 2)
    query_grid = queries.reshape(2, seq_rows, kv_local, heads_per_kv, HEAD_SIZE)
    block_rank = lax.axis_index(("ctx", "section"))
    query_pos = block_rank * seq_rows + jnp.arange(seq_rows, dtype=jnp.int32)
    last_needed = jnp.minimum(block_rank * seq_rows + seq_rows - 1, jnp.max(lengths) - 1)
    start_state = (
        jnp.full((2, kv_local, heads_per_kv, seq_rows), neg_large, jnp.float32),
        jnp.zeros((2, kv_local, heads_per_kv, seq_rows), jnp.float32),
        jnp.zeros((2, kv_local, heads_per_kv, seq_rows, HEAD_SIZE), jnp.float32),
    )
    carry_state = start_state
    kv_piece = lax.all_gather(own_pairs, ("ctx", "section"), axis=1, tiled=True)
    row_count = kv_piece.shape[1]
    block_rows = math.gcd(row_count, 512)
    blocks = jnp.moveaxis(
        kv_piece.reshape(2, row_count // block_rows, block_rows, kv_local, 2, HEAD_SIZE), 1, 0
    )

    def self_one_block(inner_state, scan_item):
        block_number, block_pairs = scan_item
        block_first = block_number * block_rows
        key_pos = block_first + jnp.arange(block_rows, dtype=jnp.int32)
        allowed = (key_pos[None, None, :] <= query_pos[None, :, None]) & (
            key_pos[None, None, :] < lengths[:, None, None]
        )

        def compute_block(state_in):
            return fold_block(
                state_in,
                query_grid,
                block_pairs[:, :, :, 0],
                block_pairs[:, :, :, 1],
                allowed[:, None, None],
                "bsgrd,bpgd->bgrsp",
                "bgrsp,bpgd->bgrsd",
            )

        def keep_state(state_in):
            return state_in

        return (lax.cond(block_first > last_needed, keep_state, compute_block, inner_state), None)

    carry_state, _ = lax.scan(
        self_one_block, carry_state, (jnp.arange(row_count // block_rows, dtype=jnp.int32), blocks)
    )
    image_rows = image_kv.shape[0]
    copies = jnp.repeat(image_kv.reshape(image_rows, KVH // kv_local, kv_cols), replicas, axis=1)
    image_own = lax.all_to_all(
        copies.reshape(image_rows, tp_count * kv_cols),
        "tp",
        split_axis=1,
        concat_axis=0,
        tiled=True,
    )
    image_carry_state = start_state
    kv_piece = lax.all_gather(image_own, ("ctx", "section"), axis=0, tiled=True)
    row_count = kv_piece.shape[0]
    image_block_rows = math.gcd(row_count, 512)
    blocks = kv_piece.reshape(
        row_count // image_block_rows, image_block_rows, kv_local, 2, HEAD_SIZE
    )
    everywhere = jnp.ones((), jnp.bool_)

    def image_one_block(inner_state, block_pairs):
        return (
            fold_block(
                inner_state,
                query_grid,
                block_pairs[:, :, 0],
                block_pairs[:, :, 1],
                everywhere,
                "bsgrd,pgd->bgrsp",
                "bgrsp,pgd->bgrsd",
            ),
            None,
        )

    image_carry_state, _ = lax.scan(image_one_block, image_carry_state, blocks)
    gate_factor = jnp.tanh(cross_gate).reshape(1, 1, kv_local, heads_per_kv, 1)
    attended = finish(carry_state) + gate_factor * finish(image_carry_state)
    return attended.reshape(2, seq_rows, heads_local * HEAD_SIZE).astype(jnp.bfloat16)


MASKED = -1e30
EXP2_SCALE = math.log2(math.e) / math.sqrt(HEAD_SIZE)
VMEM_SPEC = pl.BlockSpec(memory_space=pltpu.VMEM)
ANY_SPEC = pl.BlockSpec(memory_space=pl.ANY)
BLOCKS = 8
CHUNK = 4
KERNEL = pltpu.CompilerParams(vmem_limit_bytes=12 << 20)


def in_vmem(*arrays):
    return [pltpu.with_memory_space_constraint(array, pltpu.VMEM) for array in arrays]


def rows_by_rows(left, right):
    return lax.dot_general(left, right, (((1,), (1,)), ((), ())), preferred_element_type=jnp.float32)


def columns_by_columns(left, right):
    return lax.dot_general(left, right, (((0,), (0,)), ((), ())), preferred_element_type=jnp.float32)


def block_of(place):
    return jnp.where(place < BLOCKS // 2, place, 3 * BLOCKS // 2 - 1 - place)


def ring_blocks(shifts):
    ctx, section = lax.axis_index("ctx"), lax.axis_index("section")
    place = jnp.where(ctx == 0, section, BLOCKS - 1 - section)
    return [block_of((place + shift + BLOCKS) & (BLOCKS - 1)) for shift in shifts], ctx * (BLOCKS // 2) + section


def position_bias(block, own, limit, rows, diagonal):
    key = lax.broadcasted_iota(jnp.int32, (rows, rows), 0)
    first = jnp.where(block <= own, block * rows, 1 << 30)
    allowed = first + key < limit
    if diagonal:
        allowed &= key <= lax.broadcasted_iota(jnp.int32, (rows, rows), 1)
    return jnp.where(allowed, 0.0, MASKED)


def weigh(scores, biases, rows, old):
    if biases:
        scores = jnp.concatenate([scores[i * rows : (i + 1) * rows] + bias for i, bias in enumerate(biases)], 0)
    best = jnp.max(scores, axis=0, keepdims=True)
    if old is not None:
        best = jnp.maximum(old, best)
    weights = jnp.exp2((scores - best) * EXP2_SCALE)
    return best, jnp.sum(weights, axis=0, keepdims=True), weights.astype(jnp.bfloat16)


def weigh_heads(scores, biases, rows, heads, old):
    parts = []
    for h in range(heads):
        part = slice(h * rows, (h + 1) * rows)
        parts.append(weigh(scores[:, part], biases, rows, None if old is None else old[:, part]))
    return [jnp.concatenate(x, 1) for x in zip(*parts)]


def in_turn(units, score, weigh_unit, collect):
    ahead = score(*units[0])
    waiting = None
    for i, unit in enumerate(units):
        scores = ahead
        if i + 1 < len(units):
            ahead = score(*units[i + 1])
        weighed = weigh_unit(*unit, scores)
        if waiting is not None:
            collect(*waiting)
        waiting = (*unit, *weighed)
    collect(*waiting)


class Heads:
    def __init__(self, q_ref, groups):
        self.q_ref = q_ref
        self.sequences, self.rows = q_ref.shape[:2]
        self.heads = q_ref.shape[2] // HEAD_SIZE // groups
        self.chunk = min(CHUNK, self.heads)
        self.units = [
            (sequence, group, h)
            for group in range(groups)
            for sequence in range(self.sequences)
            for h in range(0, self.heads, self.chunk)
        ]

    def queries(self, sequence, group, h):
        first = (group * self.heads + h) * HEAD_SIZE
        columns = [slice(first + j * HEAD_SIZE, first + (j + 1) * HEAD_SIZE) for j in range(self.chunk)]
        return jnp.concatenate([self.q_ref[sequence, :, c] for c in columns], 0)

    def part(self, h):
        return slice(h * self.rows, (h + self.chunk) * self.rows)


def key_columns(group):
    return slice(2 * group * HEAD_SIZE, (2 * group + 1) * HEAD_SIZE)


def value_columns(group):
    return slice((2 * group + 1) * HEAD_SIZE, (2 * group + 2) * HEAD_SIZE)


def stack_rows(refs, sequence, columns):
    rows = [r[sequence if r.shape[0] > 1 else 0, :, columns] for r in refs]
    return jnp.concatenate(rows, 0) if len(rows) > 1 else rows[0]


def fold(heads, length_ref, blocks, numbers, own, old_state, state):
    stat_ref, sum_ref = state
    rows = heads.rows
    biases = [
        [
            position_bias(number, own, length_ref[i : i + 1], rows, old_state is None and j == 0)
            for j, number in enumerate(numbers)
        ]
        for i in range(heads.sequences)
    ]

    def score(sequence, group, h):
        return rows_by_rows(stack_rows(blocks, sequence, key_columns(group)), heads.queries(sequence, group, h))

    def weigh_unit(sequence, group, h, scores):
        part = heads.part(h)
        old = None if old_state is None else stat_ref[sequence, group, 0:1, part]
        best, total, weights = weigh_heads(scores, biases[sequence], rows, heads.chunk, old)
        shrink = None
        if old is not None:
            shrink = jnp.exp2((old - best) * EXP2_SCALE)
            total = stat_ref[sequence, group, 1:2, part] * shrink + total
        stat_ref[sequence, group, 0:1, part] = best
        stat_ref[sequence, group, 1:2, part] = total
        return shrink, weights

    def collect(sequence, group, h, shrink, weights):
        part = heads.part(h)
        added = columns_by_columns(stack_rows(blocks, sequence, value_columns(group)), weights)
        if shrink is not None:
            added = sum_ref[sequence, group, :, part] * shrink + added
        sum_ref[sequence, group, :, part] = added

    in_turn(heads.units, score, weigh_unit, collect)


def fold_useful(heads, length_ref, blocks, numbers, own, old_state, state):
    ahead = len(blocks) - 2
    useful = [number < own for number in numbers[ahead:]]

    def work(*chosen):
        chosen = [*range(ahead), *(ahead + i for i in chosen)]
        fold(heads, length_ref, [blocks[i] for i in chosen], [numbers[i] for i in chosen], own, old_state, state)

    pl.when(useful[0] & useful[1])(lambda: work(0, 1))
    pl.when(useful[1] & ~useful[0])(lambda: work(1))
    one = useful[0] | ~useful[1] if ahead else useful[0]
    pl.when(one & ~useful[1])(lambda: work(0))


def fold_kernel(first, shifts, groups, length_ref, q_ref, *refs):
    blocks = refs[: len(shifts)]
    numbers, own = ring_blocks(shifts)
    heads = Heads(q_ref, groups)
    fold_useful(heads, length_ref, blocks, numbers, own, None if first else refs[-4:-2], refs[-2:])


def state_shapes(q, groups):
    sequences, rows, columns = q.shape
    width = columns // HEAD_SIZE // groups * rows
    return [
        pltpu.VMEM((sequences, groups, 2, width), jnp.float32),
        pltpu.VMEM((sequences, groups, HEAD_SIZE, width), jnp.float32),
    ]


def cost(q, keys):
    work = q.shape[0] * q.shape[2] // HEAD_SIZE * q.shape[1] * keys
    return pl.CostEstimate(flops=work * 4 * HEAD_SIZE, bytes_accessed=1 << 20, transcendentals=work)


def fold_blocks(lengths, q, blocks, shifts, state):
    groups = blocks[0].shape[2] // (2 * HEAD_SIZE)
    first = state is None
    state = () if first else tuple(state)
    held = 2 + len(blocks)
    return pl.pallas_call(
        functools.partial(fold_kernel, first, shifts, groups),
        in_specs=[VMEM_SPEC] * (held + len(state)),
        out_specs=[VMEM_SPEC] * 2,
        out_shape=state_shapes(q, groups),
        input_output_aliases={} if first else {held + i: i for i in range(2)},
        compiler_params=KERNEL,
        cost_estimate=cost(q, q.shape[1] * len(blocks)),
        name="fold_blocks",
    )(*in_vmem(lengths, q, *blocks, *state))


def cross_kernel(groups, factor_ref, q_ref, *refs):
    images, cross_ref = refs[:-1], refs[-1]
    heads = Heads(q_ref, groups)
    rows = heads.rows
    first = lax.axis_index("tp") * 2 * groups
    columns = [pl.ds(pl.multiple_of((first + i) * HEAD_SIZE, HEAD_SIZE), HEAD_SIZE) for i in range(2 * groups)]
    image = [jnp.concatenate([r[:, c] for r in images], 0) for c in columns]

    def score(sequence, group, h):
        return rows_by_rows(image[2 * group], heads.queries(sequence, group, h))

    def weigh_unit(sequence, group, h, scores):
        _, total, weights = weigh_heads(scores, [], rows, heads.chunk, None)
        first = group * heads.heads + h
        factors = jnp.concatenate([factor_ref[first + j : first + j + 1] for j in range(heads.chunk)], 1)
        return factors / total, weights

    def collect(sequence, group, h, factors, weights):
        cross_ref[sequence, group, :, heads.part(h)] = columns_by_columns(image[2 * group + 1], weights) * factors

    in_turn(heads.units, score, weigh_unit, collect)


def cross_attend(factors, q, images, groups):
    return pl.pallas_call(
        functools.partial(cross_kernel, groups),
        in_specs=[VMEM_SPEC] * (2 + len(images)),
        out_specs=VMEM_SPEC,
        out_shape=state_shapes(q, groups)[1],
        compiler_params=KERNEL,
        cost_estimate=cost(q, q.shape[1]),
        name="cross_attend",
    )(*in_vmem(factors, q, *images))


def turned(out, rows):
    heads = [out[:, first : first + rows].T for first in range(0, out.shape[1], rows)]
    return jnp.concatenate(heads, 1).astype(jnp.bfloat16)


class Results:
    def __init__(self, heads, out_ref, held_ref, sems):
        self.heads, self.out_ref, self.held_ref, self.sems = heads, out_ref, held_ref, sems
        self.copies = []

    def put(self, sequence, group, h, out):
        heads = self.heads
        first = (group * heads.heads + h) * HEAD_SIZE
        self.held_ref[sequence, :, first : first + heads.chunk * HEAD_SIZE] = turned(out, heads.rows)
        if h + heads.chunk == heads.heads:
            width = heads.heads * HEAD_SIZE
            at = (sequence, slice(None), pl.ds(group * width, width))
            self.send(self.held_ref.at[at], at, self.sems.at[sequence, group])

    def send(self, source, at, sem):
        copy = pltpu.make_async_copy(source, self.out_ref.at[at], sem)
        copy.start()
        self.copies.append(copy)

    def wait(self):
        for copy in self.copies:
            copy.wait()


def result_scratch(q, groups):
    return [pltpu.VMEM(q.shape, q.dtype), pltpu.SemaphoreType.DMA((q.shape[0], groups))]


def early_kernel(last_shift, groups, q_ref, cross_ref, stat_ref, sum_ref, out_ref, held_ref, sems):
    (last,), own = ring_blocks([last_shift])
    heads = Heads(q_ref, groups)

    def write():
        results = Results(heads, out_ref, held_ref, sems)
        for sequence, group, h in heads.units:
            part = heads.part(h)
            over = 1.0 / stat_ref[sequence, group, 1:2, part]
            results.put(
                sequence, group, h, sum_ref[sequence, group, :, part] * over + cross_ref[sequence, group, :, part]
            )
        results.wait()

    pl.when(last > own)(write)


def early_rows(q, last_shift, groups, cross, state):
    args = in_vmem(q, cross, *state)
    return pl.pallas_call(
        functools.partial(early_kernel, last_shift, groups),
        in_specs=[VMEM_SPEC] * len(args),
        out_specs=ANY_SPEC,
        out_shape=pltpu.HBM(q.shape, q.dtype),
        scratch_shapes=result_scratch(q, groups),
        compiler_params=KERNEL,
        cost_estimate=cost(q, q.shape[1] // 4),
        name="early_rows",
    )(*args)


def last_block(heads, sequence, shift, length_ref, block, cross_ref, stat_ref, sum_ref, put):
    rows = heads.rows
    (number,), own = ring_blocks([shift])
    biases = [position_bias(number, own, length_ref[sequence : sequence + 1], rows, False)]

    def score(sequence, group, h):
        return rows_by_rows(block[0, :, key_columns(group)], heads.queries(sequence, group, h))

    def weigh_unit(sequence, group, h, scores):
        part = heads.part(h)
        old = stat_ref[sequence, group, 0:1, part]
        best, total, weights = weigh_heads(scores, biases, rows, heads.chunk, old)
        shrink = jnp.exp2((old - best) * EXP2_SCALE)
        over = 1.0 / (stat_ref[sequence, group, 1:2, part] * shrink + total)
        return shrink * over, over, weights

    def collect(sequence, group, h, old_factor, factor, weights):
        part = heads.part(h)
        added = columns_by_columns(block[0, :, value_columns(group)], weights)
        out = sum_ref[sequence, group, :, part] * old_factor + added * factor + cross_ref[sequence, group, :, part]
        put(sequence, group, h, out)

    in_turn([unit for unit in heads.units if unit[0] == sequence], score, weigh_unit, collect)


def first_finish_kernel(shift, groups, length_ref, q_ref, block, cross_ref, stat_ref, sum_ref, rows_ref):
    heads = Heads(q_ref, groups)
    (number,), own = ring_blocks([shift])

    def put(sequence, group, h, out):
        first = (group * heads.heads + h) * HEAD_SIZE
        rows_ref[:, first : first + heads.chunk * HEAD_SIZE] = turned(out, heads.rows)

    pl.when(number < own)(
        lambda: last_block(heads, 0, shift, length_ref, block, cross_ref, stat_ref, sum_ref, put)
    )


def first_finish(lengths, q, shift, block, cross, state):
    groups = block.shape[2] // (2 * HEAD_SIZE)
    args = in_vmem(lengths, q, block, cross, *state)
    return pl.pallas_call(
        functools.partial(first_finish_kernel, shift, groups),
        in_specs=[VMEM_SPEC] * len(args),
        out_specs=VMEM_SPEC,
        out_shape=pltpu.VMEM(q.shape[1:], q.dtype),
        compiler_params=KERNEL,
        cost_estimate=cost(q, q.shape[1] // 2),
        name="first_finish",
    )(*args)


def second_finish_kernel(
    shift, groups, length_ref, q_ref, block, cross_ref, stat_ref, sum_ref, rows_ref, _, out_ref, held_ref, sems
):
    heads = Heads(q_ref, groups)
    (number,), own = ring_blocks([shift])

    def work():
        results = Results(heads, out_ref, held_ref, sems)
        results.send(rows_ref, 0, sems.at[0, 0])
        last_block(heads, 1, shift, length_ref, block, cross_ref, stat_ref, sum_ref, results.put)
        results.wait()

    pl.when(number < own)(work)


def second_finish(lengths, q, shift, block, cross, state, first_rows, result):
    groups = block.shape[2] // (2 * HEAD_SIZE)
    args = in_vmem(lengths, q, block, cross, *state, first_rows)
    return pl.pallas_call(
        functools.partial(second_finish_kernel, shift, groups),
        in_specs=[VMEM_SPEC] * len(args) + [ANY_SPEC],
        out_specs=ANY_SPEC,
        out_shape=pltpu.HBM(q.shape, q.dtype),
        scratch_shapes=result_scratch(q, groups),
        input_output_aliases={len(args): 0},
        compiler_params=KERNEL,
        cost_estimate=cost(q, q.shape[1] // 2),
        name="second_finish",
    )(*args, result)


def load_kernel(lengths, gate, q_ref, image_ref, limit_ref, factor_ref, q_out, image_out, counts, gates, sems):
    pairs = ((lengths, counts), (gate, gates), (q_ref, q_out), (image_ref, image_out))
    copies = [pltpu.make_async_copy(source, target, sems.at[i]) for i, (source, target) in enumerate(pairs)]
    for copy in copies:
        copy.start()
    copies[0].wait()
    for i in range(limit_ref.shape[0]):
        limit_ref[i : i + 1] = jnp.full((1, limit_ref.shape[1]), counts[i], jnp.int32)
    copies[1].wait()
    for i in range(factor_ref.shape[0]):
        factor_ref[i : i + 1] = jnp.full((1, factor_ref.shape[1]), gates[i], jnp.float32)
    factor_ref[...] = jnp.tanh(factor_ref[...])
    copies[2].wait()
    copies[3].wait()


def load_inputs(*arrays):
    lengths, gate, q, image = arrays
    rows = q.shape[1]
    return pl.pallas_call(
        load_kernel,
        in_specs=[ANY_SPEC] * 4,
        out_specs=[VMEM_SPEC] * 4,
        out_shape=[
            pltpu.VMEM((lengths.shape[0], rows), jnp.int32),
            pltpu.VMEM((gate.shape[0], rows), jnp.float32),
            pltpu.VMEM(q.shape, q.dtype),
            pltpu.VMEM(image.shape, image.dtype),
        ],
        scratch_shapes=[
            pltpu.SMEM(lengths.shape, lengths.dtype),
            pltpu.SMEM(gate.shape, gate.dtype),
            pltpu.SemaphoreType.DMA((4,)),
        ],
        compiler_params=KERNEL,
        name="load_inputs",
    )(*[pltpu.with_memory_space_constraint(array, pltpu.HBM) for array in arrays])


def join_kernel(first_ref, second_ref, joined_ref):
    rows = [r[...].astype(jnp.float32) for r in (first_ref, second_ref)]
    joined_ref[...] = jnp.concatenate(rows, 0).astype(joined_ref.dtype)


def joined(first, second):
    return pl.pallas_call(
        join_kernel,
        in_specs=[VMEM_SPEC] * 2,
        out_specs=VMEM_SPEC,
        out_shape=pltpu.VMEM((first.shape[0] + second.shape[0], first.shape[1]), first.dtype),
        compiler_params=KERNEL,
        name="joined",
    )(*in_vmem(first, second))


def half_kernel(sequence, block_ref, half_ref):
    half_ref[...] = block_ref[sequence : sequence + 1]


def half_of(block, sequence):
    return pl.pallas_call(
        functools.partial(half_kernel, sequence),
        in_specs=[VMEM_SPEC],
        out_specs=VMEM_SPEC,
        out_shape=pltpu.VMEM((1,) + block.shape[1:], block.dtype),
        compiler_params=KERNEL,
        name="half_of",
    )(*in_vmem(block))


RING = (0, 1, 2, 3, 7, 6, 5, 4)


def ring_forward(block):
    pairs = [(RING[i], RING[(i + 1) % BLOCKS]) for i in range(BLOCKS)]
    return lax.ppermute(block, ("ctx", "section"), pairs)


def ring_backward(block):
    pairs = [(RING[(i + 1) % BLOCKS], RING[i]) for i in range(BLOCKS)]
    return lax.ppermute(block, ("ctx", "section"), pairs)


def after(block, *others):
    return lax.optimization_barrier((block,) + others)[0]


def swapped(rows, name, bits):
    return lax.ppermute(rows, name, [(i, i ^ bits) for i in range(lax.axis_size(name))])


def ring_device(queries, self_kv, image_kv, cross_gate, lengths):
    tp_count = lax.axis_size("tp")
    groups = KVH // tp_count
    kv_cols = groups * 2 * HEAD_SIZE
    own = lax.dynamic_slice_in_dim(self_kv, lax.axis_index("tp") * kv_cols, kv_cols, 2)
    f1, b1 = ring_forward(own), ring_backward(own)
    sections = lax.axis_size("section")
    n1 = swapped(image_kv, "section", 2)
    n2 = swapped(image_kv, "ctx", 1)
    n3 = swapped(image_kv, ("ctx", "section"), sections + 2)
    limits, factors, q, image1 = load_inputs(lengths, cross_gate, queries, image_kv)

    f2, b2 = ring_forward(f1), ring_backward(b1)
    image4 = jnp.concatenate([image1, n1, n2, n3], 0)
    far = swapped(image4, "section", 1)
    state = fold_blocks(limits, q, [own, f1, after(b1, image4)], (0, -1, 1), None)

    f3, b3 = ring_forward(after(f2, state[0], far)), ring_backward(after(b2, state[0], far))
    image8 = joined(image4, far)
    images = [image8] + [swapped(image8, "tp", bits) for bits in range(1, tp_count)]
    state = fold_blocks(limits, q, [f2, after(b2, image8)], (-2, 2), state)

    f4 = ring_forward(half_of(after(f3, state[0]), 0))
    b4 = ring_backward(half_of(after(b3, state[0], *images), 1))
    cross = cross_attend(factors, q, images, groups)
    state = fold_blocks(limits, q, [f3, b3], (-3, 3), state)
    result = early_rows(q, 4, groups, cross, state)
    first_rows = first_finish(limits, q, 4, f4, cross, state)
    return second_finish(limits, q, 4, b4, cross, state, first_rows, result)


def solution(mesh):
    placed = (
        P(None, ("ctx", "section"), "tp"),
        P(None, ("ctx", "section"), None),
        P(("ctx", "tp", "section"), None),
        P("tp"),
        P(),
    )
    ring = mesh.shape["ctx"] == 2 and mesh.shape["section"] == 4 and mesh.shape["tp"] == 4
    return jax.shard_map(
        ring_device if ring else scan_device,
        mesh=mesh,
        in_specs=placed,
        out_specs=P(None, ("ctx", "section"), "tp"),
        check_vma=False,
    )
```

```python
import functools
import math

import jax
import jax.numpy as jnp
from jax import lax
from jax.experimental import pallas as pl
from jax.experimental.pallas import tpu as pltpu
from jax.sharding import PartitionSpec as P

HQ = 64
KVH = 8
HEAD_SIZE = 128


neg_large = -1e30


def fold_block(carry_state, query_grid, key_matrix, value_matrix, allowed, score_form, value_form):
    row_best, row_total, weighted = carry_state
    logit_scores = jnp.einsum(
        score_form, query_grid, key_matrix, preferred_element_type=jnp.float32
    ) * (1.0 / math.sqrt(HEAD_SIZE))
    masked = jnp.where(allowed, logit_scores, neg_large)
    new_best = jnp.maximum(row_best, jnp.max(masked, axis=-1))
    weights = jnp.where(allowed, jnp.exp(masked - new_best[..., None]), 0.0)
    shrink = jnp.exp(row_best - new_best)
    row_total = row_total * shrink + jnp.sum(weights, axis=-1)
    weighted = weighted * shrink[..., None] + jnp.einsum(
        value_form, weights.astype(jnp.bfloat16), value_matrix, preferred_element_type=jnp.float32
    )
    return (new_best, row_total, weighted)


def finish(carry_state):
    return jnp.transpose(carry_state[2] / carry_state[1][..., None], (0, 3, 1, 2, 4))


def scan_device(queries, self_kv, image_kv, cross_gate, lengths):
    tp_count = lax.axis_size("tp")
    heads_local = HQ // tp_count
    kv_local = max(1, KVH // tp_count)
    replicas = max(1, tp_count // KVH)
    heads_per_kv = heads_local // kv_local
    seq_rows = queries.shape[1]
    kv_cols = kv_local * 2 * HEAD_SIZE
    tp_rank = lax.axis_index("tp")
    own_pairs = lax.dynamic_slice_in_dim(self_kv, tp_rank // replicas * kv_cols, kv_cols, 2)
    query_grid = queries.reshape(2, seq_rows, kv_local, heads_per_kv, HEAD_SIZE)
    block_rank = lax.axis_index(("ctx", "section"))
    query_pos = block_rank * seq_rows + jnp.arange(seq_rows, dtype=jnp.int32)
    last_needed = jnp.minimum(block_rank * seq_rows + seq_rows - 1, jnp.max(lengths) - 1)
    start_state = (
        jnp.full((2, kv_local, heads_per_kv, seq_rows), neg_large, jnp.float32),
        jnp.zeros((2, kv_local, heads_per_kv, seq_rows), jnp.float32),
        jnp.zeros((2, kv_local, heads_per_kv, seq_rows, HEAD_SIZE), jnp.float32),
    )
    carry_state = start_state
    kv_piece = lax.all_gather(own_pairs, ("ctx", "section"), axis=1, tiled=True)
    row_count = kv_piece.shape[1]
    block_rows = math.gcd(row_count, 512)
    blocks = jnp.moveaxis(
        kv_piece.reshape(2, row_count // block_rows, block_rows, kv_local, 2, HEAD_SIZE), 1, 0
    )

    def self_one_block(inner_state, scan_item):
        block_number, block_pairs = scan_item
        block_first = block_number * block_rows
        key_pos = block_first + jnp.arange(block_rows, dtype=jnp.int32)
        allowed = (key_pos[None, None, :] <= query_pos[None, :, None]) & (
            key_pos[None, None, :] < lengths[:, None, None]
        )

        def compute_block(state_in):
            return fold_block(
                state_in,
                query_grid,
                block_pairs[:, :, :, 0],
                block_pairs[:, :, :, 1],
                allowed[:, None, None],
                "bsgrd,bpgd->bgrsp",
                "bgrsp,bpgd->bgrsd",
            )

        def keep_state(state_in):
            return state_in

        return (lax.cond(block_first > last_needed, keep_state, compute_block, inner_state), None)

    carry_state, _ = lax.scan(
        self_one_block, carry_state, (jnp.arange(row_count // block_rows, dtype=jnp.int32), blocks)
    )
    image_rows = image_kv.shape[0]
    copies = jnp.repeat(image_kv.reshape(image_rows, KVH // kv_local, kv_cols), replicas, axis=1)
    image_own = lax.all_to_all(
        copies.reshape(image_rows, tp_count * kv_cols),
        "tp",
        split_axis=1,
        concat_axis=0,
        tiled=True,
    )
    image_carry_state = start_state
    kv_piece = lax.all_gather(image_own, ("ctx", "section"), axis=0, tiled=True)
    row_count = kv_piece.shape[0]
    image_block_rows = math.gcd(row_count, 512)
    blocks = kv_piece.reshape(
        row_count // image_block_rows, image_block_rows, kv_local, 2, HEAD_SIZE
    )
    everywhere = jnp.ones((), jnp.bool_)

    def image_one_block(inner_state, block_pairs):
        return (
            fold_block(
                inner_state,
                query_grid,
                block_pairs[:, :, 0],
                block_pairs[:, :, 1],
                everywhere,
                "bsgrd,pgd->bgrsp",
                "bgrsp,pgd->bgrsd",
            ),
            None,
        )

    image_carry_state, _ = lax.scan(image_one_block, image_carry_state, blocks)
    gate_factor = jnp.tanh(cross_gate).reshape(1, 1, kv_local, heads_per_kv, 1)
    attended = finish(carry_state) + gate_factor * finish(image_carry_state)
    return attended.reshape(2, seq_rows, heads_local * HEAD_SIZE).astype(jnp.bfloat16)


MASKED = -1e30
EXP2_SCALE = math.log2(math.e) / math.sqrt(HEAD_SIZE)
VMEM_SPEC = pl.BlockSpec(memory_space=pltpu.VMEM)
ANY_SPEC = pl.BlockSpec(memory_space=pl.ANY)
BLOCKS = 8
CHUNK = 8
KERNEL = pltpu.CompilerParams(vmem_limit_bytes=12 << 20)


def in_vmem(*arrays):
    return [pltpu.with_memory_space_constraint(array, pltpu.VMEM) for array in arrays]


def rows_by_rows(left, right):
    return lax.dot_general(left, right, (((1,), (1,)), ((), ())), preferred_element_type=jnp.float32)


def columns_by_columns(left, right):
    return lax.dot_general(left, right, (((0,), (0,)), ((), ())), preferred_element_type=jnp.float32)


def block_of(place):
    return jnp.where(place < BLOCKS // 2, place, 3 * BLOCKS // 2 - 1 - place)


def ring_blocks(shifts):
    ctx, section = lax.axis_index("ctx"), lax.axis_index("section")
    place = jnp.where(ctx == 0, section, BLOCKS - 1 - section)
    return [block_of((place + shift + BLOCKS) & (BLOCKS - 1)) for shift in shifts], ctx * (BLOCKS // 2) + section


def position_bias(block, own, limit, rows, diagonal):
    key = lax.broadcasted_iota(jnp.int32, (rows, rows), 0)
    first = jnp.where(block <= own, block * rows, 1 << 30)
    allowed = first + key < limit
    if diagonal:
        allowed &= key <= lax.broadcasted_iota(jnp.int32, (rows, rows), 1)
    return jnp.where(allowed, 0.0, MASKED)


def weigh(scores, biases, rows, old):
    if biases:
        scores = jnp.concatenate([scores[i * rows : (i + 1) * rows] + bias for i, bias in enumerate(biases)], 0)
    best = jnp.max(scores, axis=0, keepdims=True)
    if old is not None:
        best = jnp.maximum(old, best)
    weights = jnp.exp2((scores - best) * EXP2_SCALE)
    return best, jnp.sum(weights, axis=0, keepdims=True), weights.astype(jnp.bfloat16)


def weigh_heads(scores, biases, rows, heads, old):
    parts = []
    for h in range(heads):
        part = slice(h * rows, (h + 1) * rows)
        parts.append(weigh(scores[:, part], biases, rows, None if old is None else old[:, part]))
    return [jnp.concatenate(x, 1) for x in zip(*parts)]


def in_turn(units, score, weigh_unit, collect):
    ahead = score(*units[0])
    waiting = None
    for i, unit in enumerate(units):
        scores = ahead
        if i + 1 < len(units):
            ahead = score(*units[i + 1])
        weighed = weigh_unit(*unit, scores)
        if waiting is not None:
            collect(*waiting)
        waiting = (*unit, *weighed)
    collect(*waiting)


class Heads:
    def __init__(self, q_ref, groups):
        self.q_ref = q_ref
        self.sequences, self.rows = q_ref.shape[:2]
        self.heads = q_ref.shape[2] // HEAD_SIZE // groups
        self.chunk = min(CHUNK, self.heads)
        self.units = [
            (sequence, group, h)
            for group in range(groups)
            for sequence in range(self.sequences)
            for h in range(0, self.heads, self.chunk)
        ]

    def queries(self, sequence, group, h):
        first = (group * self.heads + h) * HEAD_SIZE
        columns = [slice(first + j * HEAD_SIZE, first + (j + 1) * HEAD_SIZE) for j in range(self.chunk)]
        return jnp.concatenate([self.q_ref[sequence, :, c] for c in columns], 0)

    def part(self, h):
        return slice(h * self.rows, (h + self.chunk) * self.rows)


def key_columns(group):
    return slice(2 * group * HEAD_SIZE, (2 * group + 1) * HEAD_SIZE)


def value_columns(group):
    return slice((2 * group + 1) * HEAD_SIZE, (2 * group + 2) * HEAD_SIZE)


def stack_rows(refs, sequence, columns):
    rows = [r[sequence if r.shape[0] > 1 else 0, :, columns] for r in refs]
    return jnp.concatenate(rows, 0) if len(rows) > 1 else rows[0]


def fold(heads, length_ref, blocks, numbers, own, old_state, state):
    stat_ref, sum_ref = state
    rows = heads.rows
    biases = [
        [
            position_bias(number, own, length_ref[i : i + 1], rows, old_state is None and j == 0)
            for j, number in enumerate(numbers)
        ]
        for i in range(heads.sequences)
    ]

    def score(sequence, group, h):
        return rows_by_rows(stack_rows(blocks, sequence, key_columns(group)), heads.queries(sequence, group, h))

    def weigh_unit(sequence, group, h, scores):
        part = heads.part(h)
        old = None if old_state is None else stat_ref[sequence, group, 0:1, part]
        best, total, weights = weigh_heads(scores, biases[sequence], rows, heads.chunk, old)
        shrink = None
        if old is not None:
            shrink = jnp.exp2((old - best) * EXP2_SCALE)
            total = stat_ref[sequence, group, 1:2, part] * shrink + total
        stat_ref[sequence, group, 0:1, part] = best
        stat_ref[sequence, group, 1:2, part] = total
        return shrink, weights

    def collect(sequence, group, h, shrink, weights):
        part = heads.part(h)
        added = columns_by_columns(stack_rows(blocks, sequence, value_columns(group)), weights)
        if shrink is not None:
            added = sum_ref[sequence, group, :, part] * shrink + added
        sum_ref[sequence, group, :, part] = added

    in_turn(heads.units, score, weigh_unit, collect)


def fold_useful(heads, length_ref, blocks, numbers, own, old_state, state):
    ahead = len(blocks) - 2
    useful = [number < own for number in numbers[ahead:]]

    def work(*chosen):
        chosen = [*range(ahead), *(ahead + i for i in chosen)]
        fold(heads, length_ref, [blocks[i] for i in chosen], [numbers[i] for i in chosen], own, old_state, state)

    pl.when(useful[0] & useful[1])(lambda: work(0, 1))
    pl.when(useful[1] & ~useful[0])(lambda: work(1))
    one = useful[0] | ~useful[1] if ahead else useful[0]
    pl.when(one & ~useful[1])(lambda: work(0))


def fold_kernel(first, shifts, groups, length_ref, q_ref, *refs):
    blocks = refs[: len(shifts)]
    numbers, own = ring_blocks(shifts)
    heads = Heads(q_ref, groups)
    fold_useful(heads, length_ref, blocks, numbers, own, None if first else refs[-4:-2], refs[-2:])


def state_shapes(q, groups):
    sequences, rows, columns = q.shape
    width = columns // HEAD_SIZE // groups * rows
    return [
        pltpu.VMEM((sequences, groups, 2, width), jnp.float32),
        pltpu.VMEM((sequences, groups, HEAD_SIZE, width), jnp.float32),
    ]


def cost(q, keys):
    work = q.shape[0] * q.shape[2] // HEAD_SIZE * q.shape[1] * keys
    return pl.CostEstimate(flops=work * 4 * HEAD_SIZE, bytes_accessed=1 << 20, transcendentals=work)


def fold_blocks(lengths, q, blocks, shifts, state):
    groups = blocks[0].shape[2] // (2 * HEAD_SIZE)
    first = state is None
    state = () if first else tuple(state)
    held = 2 + len(blocks)
    return pl.pallas_call(
        functools.partial(fold_kernel, first, shifts, groups),
        in_specs=[VMEM_SPEC] * (held + len(state)),
        out_specs=[VMEM_SPEC] * 2,
        out_shape=state_shapes(q, groups),
        input_output_aliases={} if first else {held + i: i for i in range(2)},
        compiler_params=KERNEL,
        cost_estimate=cost(q, q.shape[1] * len(blocks)),
        name="fold_blocks",
    )(*in_vmem(lengths, q, *blocks, *state))


def cross_kernel(groups, factor_ref, q_ref, *refs):
    images, cross_ref = refs[:-1], refs[-1]
    heads = Heads(q_ref, groups)
    rows = heads.rows
    first = lax.axis_index("tp") * 2 * groups
    columns = [pl.ds(pl.multiple_of((first + i) * HEAD_SIZE, HEAD_SIZE), HEAD_SIZE) for i in range(2 * groups)]
    image = [jnp.concatenate([r[:, c] for r in images], 0) for c in columns]

    def score(sequence, group, h):
        return rows_by_rows(image[2 * group], heads.queries(sequence, group, h))

    def weigh_unit(sequence, group, h, scores):
        _, total, weights = weigh_heads(scores, [], rows, heads.chunk, None)
        first = group * heads.heads + h
        factors = jnp.concatenate([factor_ref[first + j : first + j + 1] for j in range(heads.chunk)], 1)
        return factors / total, weights

    def collect(sequence, group, h, factors, weights):
        cross_ref[sequence, group, :, heads.part(h)] = columns_by_columns(image[2 * group + 1], weights) * factors

    in_turn(heads.units, score, weigh_unit, collect)


def cross_attend(factors, q, images, groups):
    return pl.pallas_call(
        functools.partial(cross_kernel, groups),
        in_specs=[VMEM_SPEC] * (2 + len(images)),
        out_specs=VMEM_SPEC,
        out_shape=state_shapes(q, groups)[1],
        compiler_params=KERNEL,
        cost_estimate=cost(q, q.shape[1]),
        name="cross_attend",
    )(*in_vmem(factors, q, *images))


def turned(out, rows):
    heads = [out[:, first : first + rows].T for first in range(0, out.shape[1], rows)]
    return jnp.concatenate(heads, 1).astype(jnp.bfloat16)


class Results:
    def __init__(self, heads, out_ref, held_ref, sems):
        self.heads, self.out_ref, self.held_ref, self.sems = heads, out_ref, held_ref, sems
        self.copies = []

    def put(self, sequence, group, h, out):
        heads = self.heads
        first = (group * heads.heads + h) * HEAD_SIZE
        self.held_ref[sequence, :, first : first + heads.chunk * HEAD_SIZE] = turned(out, heads.rows)
        if h + heads.chunk == heads.heads:
            width = heads.heads * HEAD_SIZE
            at = (sequence, slice(None), pl.ds(group * width, width))
            self.send(self.held_ref.at[at], at, self.sems.at[sequence, group])

    def send(self, source, at, sem):
        copy = pltpu.make_async_copy(source, self.out_ref.at[at], sem)
        copy.start()
        self.copies.append(copy)

    def wait(self):
        for copy in self.copies:
            copy.wait()


def result_scratch(q, groups):
    return [pltpu.VMEM(q.shape, q.dtype), pltpu.SemaphoreType.DMA((q.shape[0], groups))]


def early_kernel(last_shift, groups, q_ref, cross_ref, stat_ref, sum_ref, out_ref, held_ref, sems):
    (last,), own = ring_blocks([last_shift])
    heads = Heads(q_ref, groups)

    def write():
        results = Results(heads, out_ref, held_ref, sems)
        for sequence, group, h in heads.units:
            part = heads.part(h)
            over = 1.0 / stat_ref[sequence, group, 1:2, part]
            results.put(
                sequence, group, h, sum_ref[sequence, group, :, part] * over + cross_ref[sequence, group, :, part]
            )
        results.wait()

    pl.when(last > own)(write)


def early_rows(q, last_shift, groups, cross, state):
    args = in_vmem(q, cross, *state)
    return pl.pallas_call(
        functools.partial(early_kernel, last_shift, groups),
        in_specs=[VMEM_SPEC] * len(args),
        out_specs=ANY_SPEC,
        out_shape=pltpu.HBM(q.shape, q.dtype),
        scratch_shapes=result_scratch(q, groups),
        compiler_params=KERNEL,
        cost_estimate=cost(q, q.shape[1] // 4),
        name="early_rows",
    )(*args)


def last_block(heads, sequence, shift, length_ref, block, cross_ref, stat_ref, sum_ref, put):
    rows = heads.rows
    (number,), own = ring_blocks([shift])
    biases = [position_bias(number, own, length_ref[sequence : sequence + 1], rows, False)]

    def score(sequence, group, h):
        return rows_by_rows(block[0, :, key_columns(group)], heads.queries(sequence, group, h))

    def weigh_unit(sequence, group, h, scores):
        part = heads.part(h)
        old = stat_ref[sequence, group, 0:1, part]
        best, total, weights = weigh_heads(scores, biases, rows, heads.chunk, old)
        shrink = jnp.exp2((old - best) * EXP2_SCALE)
        over = 1.0 / (stat_ref[sequence, group, 1:2, part] * shrink + total)
        return shrink * over, over, weights

    def collect(sequence, group, h, old_factor, factor, weights):
        part = heads.part(h)
        added = columns_by_columns(block[0, :, value_columns(group)], weights)
        out = sum_ref[sequence, group, :, part] * old_factor + added * factor + cross_ref[sequence, group, :, part]
        put(sequence, group, h, out)

    in_turn([unit for unit in heads.units if unit[0] == sequence], score, weigh_unit, collect)


def first_finish_kernel(shift, groups, length_ref, q_ref, block, cross_ref, stat_ref, sum_ref, rows_ref):
    heads = Heads(q_ref, groups)
    (number,), own = ring_blocks([shift])

    def put(sequence, group, h, out):
        first = (group * heads.heads + h) * HEAD_SIZE
        rows_ref[:, first : first + heads.chunk * HEAD_SIZE] = turned(out, heads.rows)

    pl.when(number < own)(
        lambda: last_block(heads, 0, shift, length_ref, block, cross_ref, stat_ref, sum_ref, put)
    )


def first_finish(lengths, q, shift, block, cross, state):
    groups = block.shape[2] // (2 * HEAD_SIZE)
    args = in_vmem(lengths, q, block, cross, *state)
    return pl.pallas_call(
        functools.partial(first_finish_kernel, shift, groups),
        in_specs=[VMEM_SPEC] * len(args),
        out_specs=VMEM_SPEC,
        out_shape=pltpu.VMEM(q.shape[1:], q.dtype),
        compiler_params=KERNEL,
        cost_estimate=cost(q, q.shape[1] // 2),
        name="first_finish",
    )(*args)


def second_finish_kernel(
    shift, groups, length_ref, q_ref, block, cross_ref, stat_ref, sum_ref, rows_ref, _, out_ref, held_ref, sems
):
    heads = Heads(q_ref, groups)
    (number,), own = ring_blocks([shift])

    def work():
        results = Results(heads, out_ref, held_ref, sems)
        results.send(rows_ref, 0, sems.at[0, 0])
        last_block(heads, 1, shift, length_ref, block, cross_ref, stat_ref, sum_ref, results.put)
        results.wait()

    pl.when(number < own)(work)


def second_finish(lengths, q, shift, block, cross, state, first_rows, result):
    groups = block.shape[2] // (2 * HEAD_SIZE)
    args = in_vmem(lengths, q, block, cross, *state, first_rows)
    return pl.pallas_call(
        functools.partial(second_finish_kernel, shift, groups),
        in_specs=[VMEM_SPEC] * len(args) + [ANY_SPEC],
        out_specs=ANY_SPEC,
        out_shape=pltpu.HBM(q.shape, q.dtype),
        scratch_shapes=result_scratch(q, groups),
        input_output_aliases={len(args): 0},
        compiler_params=KERNEL,
        cost_estimate=cost(q, q.shape[1] // 2),
        name="second_finish",
    )(*args, result)


def load_kernel(parity, lengths, gate, q_ref, image_ref, *refs):
    limit_ref, factor_ref, q_out, image_out, counts, gates, sems = refs[-7:]

    def work():
        pairs = ((lengths, counts), (gate, gates), (q_ref, q_out), (image_ref, image_out))
        copies = [pltpu.make_async_copy(source, target, sems.at[i]) for i, (source, target) in enumerate(pairs)]
        for copy in copies:
            copy.start()
        copies[0].wait()
        for i in range(limit_ref.shape[0]):
            limit_ref[i : i + 1] = jnp.full((1, limit_ref.shape[1]), counts[i], jnp.int32)
        copies[1].wait()
        for i in range(factor_ref.shape[0]):
            factor_ref[i : i + 1] = jnp.full((1, factor_ref.shape[1]), gates[i], jnp.float32)
        factor_ref[...] = jnp.tanh(factor_ref[...])
        copies[2].wait()
        copies[3].wait()

    pl.when((lax.axis_index("tp") & 1) == parity)(work)


def load_inputs(parity, loaded, *arrays):
    lengths, gate, q, image = arrays
    rows = q.shape[1]
    return pl.pallas_call(
        functools.partial(load_kernel, parity),
        in_specs=[ANY_SPEC] * 4 + [VMEM_SPEC] * len(loaded),
        out_specs=[VMEM_SPEC] * 4,
        out_shape=[
            pltpu.VMEM((lengths.shape[0], rows), jnp.int32),
            pltpu.VMEM((gate.shape[0], rows), jnp.float32),
            pltpu.VMEM(q.shape, q.dtype),
            pltpu.VMEM(image.shape, image.dtype),
        ],
        scratch_shapes=[
            pltpu.SMEM(lengths.shape, lengths.dtype),
            pltpu.SMEM(gate.shape, gate.dtype),
            pltpu.SemaphoreType.DMA((4,)),
        ],
        input_output_aliases={4 + i: i for i in range(len(loaded))},
        compiler_params=KERNEL,
        name="load_inputs",
    )(*[pltpu.with_memory_space_constraint(array, pltpu.HBM) for array in arrays], *in_vmem(*loaded))


def join_kernel(first_ref, second_ref, joined_ref):
    rows = [r[...].astype(jnp.float32) for r in (first_ref, second_ref)]
    joined_ref[...] = jnp.concatenate(rows, 0).astype(joined_ref.dtype)


def joined(first, second):
    return pl.pallas_call(
        join_kernel,
        in_specs=[VMEM_SPEC] * 2,
        out_specs=VMEM_SPEC,
        out_shape=pltpu.VMEM((first.shape[0] + second.shape[0], first.shape[1]), first.dtype),
        compiler_params=KERNEL,
        name="joined",
    )(*in_vmem(first, second))


def half_kernel(sequence, block_ref, half_ref):
    half_ref[...] = block_ref[sequence : sequence + 1]


def half_of(block, sequence):
    return pl.pallas_call(
        functools.partial(half_kernel, sequence),
        in_specs=[VMEM_SPEC],
        out_specs=VMEM_SPEC,
        out_shape=pltpu.VMEM((1,) + block.shape[1:], block.dtype),
        compiler_params=KERNEL,
        name="half_of",
    )(*in_vmem(block))


RING = (0, 1, 2, 3, 7, 6, 5, 4)


def ring_forward(block):
    pairs = [(RING[i], RING[(i + 1) % BLOCKS]) for i in range(BLOCKS)]
    return lax.ppermute(block, ("ctx", "section"), pairs)


def ring_backward(block):
    pairs = [(RING[(i + 1) % BLOCKS], RING[i]) for i in range(BLOCKS)]
    return lax.ppermute(block, ("ctx", "section"), pairs)


def after(block, *others):
    return lax.optimization_barrier((block,) + others)[0]


def swapped(rows, name, bits):
    return lax.ppermute(rows, name, [(i, i ^ bits) for i in range(lax.axis_size(name))])


def ring_device(queries, self_kv, image_kv, cross_gate, lengths):
    tp_count = lax.axis_size("tp")
    groups = KVH // tp_count
    kv_cols = groups * 2 * HEAD_SIZE
    own = lax.dynamic_slice_in_dim(self_kv, lax.axis_index("tp") * kv_cols, kv_cols, 2)
    loaded = load_inputs(0, (), lengths, cross_gate, queries, image_kv)
    own = after(own, loaded[0])
    f1, b1 = ring_forward(own), ring_backward(own)
    sections = lax.axis_size("section")
    n1 = swapped(image_kv, "section", 2)
    n2 = swapped(image_kv, "ctx", 1)
    n3 = swapped(image_kv, ("ctx", "section"), sections + 2)
    limits, factors, q, image1 = load_inputs(1, tuple(loaded), lengths, cross_gate, queries, image_kv)

    f2, b2 = ring_forward(f1), ring_backward(b1)
    image4 = jnp.concatenate([image1, n1, n2, n3], 0)
    far = swapped(image4, "section", 1)
    state = fold_blocks(limits, q, [own, f1, after(b1, image4)], (0, -1, 1), None)

    f3, b3 = ring_forward(after(f2, state[0])), ring_backward(after(b2, state[0], far))
    image8 = joined(image4, far)
    images = [image8] + [swapped(image8, "tp", bits) for bits in range(1, tp_count)]
    state = fold_blocks(limits, q, [f2, after(b2, image8)], (-2, 2), state)

    f4 = ring_forward(half_of(after(f3, state[0]), 0))
    b4 = ring_backward(half_of(after(b3, state[0], *images), 1))
    cross = cross_attend(factors, q, images, groups)
    state = fold_blocks(limits, q, [f3, b3], (-3, 3), state)
    result = early_rows(q, 4, groups, cross, state)
    first_rows = first_finish(limits, q, 4, f4, cross, state)
    return second_finish(limits, q, 4, b4, cross, state, first_rows, result)


def solution(mesh):
    placed = (
        P(None, ("ctx", "section"), "tp"),
        P(None, ("ctx", "section"), None),
        P(("ctx", "tp", "section"), None),
        P("tp"),
        P(),
    )
    ring = mesh.shape["ctx"] == 2 and mesh.shape["section"] == 4 and mesh.shape["tp"] == 4
    return jax.shard_map(
        ring_device if ring else scan_device,
        mesh=mesh,
        in_specs=placed,
        out_specs=P(None, ("ctx", "section"), "tp"),
        check_vma=False,
    )
```

```python
import functools
import math

import jax
import jax.numpy as jnp
from jax import lax
from jax.experimental import pallas as pl
from jax.experimental.pallas import tpu as pltpu
from jax.sharding import PartitionSpec as P

HQ = 64
KVH = 8
HEAD_SIZE = 128


neg_large = -1e30


def fold_block(carry_state, query_grid, key_matrix, value_matrix, allowed, score_form, value_form):
    row_best, row_total, weighted = carry_state
    logit_scores = jnp.einsum(
        score_form, query_grid, key_matrix, preferred_element_type=jnp.float32
    ) * (1.0 / math.sqrt(HEAD_SIZE))
    masked = jnp.where(allowed, logit_scores, neg_large)
    new_best = jnp.maximum(row_best, jnp.max(masked, axis=-1))
    weights = jnp.where(allowed, jnp.exp(masked - new_best[..., None]), 0.0)
    shrink = jnp.exp(row_best - new_best)
    row_total = row_total * shrink + jnp.sum(weights, axis=-1)
    weighted = weighted * shrink[..., None] + jnp.einsum(
        value_form, weights.astype(jnp.bfloat16), value_matrix, preferred_element_type=jnp.float32
    )
    return (new_best, row_total, weighted)


def finish(carry_state):
    return jnp.transpose(carry_state[2] / carry_state[1][..., None], (0, 3, 1, 2, 4))


def scan_device(queries, self_kv, image_kv, cross_gate, lengths):
    tp_count = lax.axis_size("tp")
    heads_local = HQ // tp_count
    kv_local = max(1, KVH // tp_count)
    replicas = max(1, tp_count // KVH)
    heads_per_kv = heads_local // kv_local
    seq_rows = queries.shape[1]
    kv_cols = kv_local * 2 * HEAD_SIZE
    tp_rank = lax.axis_index("tp")
    own_pairs = lax.dynamic_slice_in_dim(self_kv, tp_rank // replicas * kv_cols, kv_cols, 2)
    query_grid = queries.reshape(2, seq_rows, kv_local, heads_per_kv, HEAD_SIZE)
    block_rank = lax.axis_index(("ctx", "section"))
    query_pos = block_rank * seq_rows + jnp.arange(seq_rows, dtype=jnp.int32)
    last_needed = jnp.minimum(block_rank * seq_rows + seq_rows - 1, jnp.max(lengths) - 1)
    start_state = (
        jnp.full((2, kv_local, heads_per_kv, seq_rows), neg_large, jnp.float32),
        jnp.zeros((2, kv_local, heads_per_kv, seq_rows), jnp.float32),
        jnp.zeros((2, kv_local, heads_per_kv, seq_rows, HEAD_SIZE), jnp.float32),
    )
    carry_state = start_state
    kv_piece = lax.all_gather(own_pairs, ("ctx", "section"), axis=1, tiled=True)
    row_count = kv_piece.shape[1]
    block_rows = math.gcd(row_count, 512)
    blocks = jnp.moveaxis(
        kv_piece.reshape(2, row_count // block_rows, block_rows, kv_local, 2, HEAD_SIZE), 1, 0
    )

    def self_one_block(inner_state, scan_item):
        block_number, block_pairs = scan_item
        block_first = block_number * block_rows
        key_pos = block_first + jnp.arange(block_rows, dtype=jnp.int32)
        allowed = (key_pos[None, None, :] <= query_pos[None, :, None]) & (
            key_pos[None, None, :] < lengths[:, None, None]
        )

        def compute_block(state_in):
            return fold_block(
                state_in,
                query_grid,
                block_pairs[:, :, :, 0],
                block_pairs[:, :, :, 1],
                allowed[:, None, None],
                "bsgrd,bpgd->bgrsp",
                "bgrsp,bpgd->bgrsd",
            )

        def keep_state(state_in):
            return state_in

        return (lax.cond(block_first > last_needed, keep_state, compute_block, inner_state), None)

    carry_state, _ = lax.scan(
        self_one_block, carry_state, (jnp.arange(row_count // block_rows, dtype=jnp.int32), blocks)
    )
    image_rows = image_kv.shape[0]
    copies = jnp.repeat(image_kv.reshape(image_rows, KVH // kv_local, kv_cols), replicas, axis=1)
    image_own = lax.all_to_all(
        copies.reshape(image_rows, tp_count * kv_cols),
        "tp",
        split_axis=1,
        concat_axis=0,
        tiled=True,
    )
    image_carry_state = start_state
    kv_piece = lax.all_gather(image_own, ("ctx", "section"), axis=0, tiled=True)
    row_count = kv_piece.shape[0]
    image_block_rows = math.gcd(row_count, 512)
    blocks = kv_piece.reshape(
        row_count // image_block_rows, image_block_rows, kv_local, 2, HEAD_SIZE
    )
    everywhere = jnp.ones((), jnp.bool_)

    def image_one_block(inner_state, block_pairs):
        return (
            fold_block(
                inner_state,
                query_grid,
                block_pairs[:, :, 0],
                block_pairs[:, :, 1],
                everywhere,
                "bsgrd,pgd->bgrsp",
                "bgrsp,pgd->bgrsd",
            ),
            None,
        )

    image_carry_state, _ = lax.scan(image_one_block, image_carry_state, blocks)
    gate_factor = jnp.tanh(cross_gate).reshape(1, 1, kv_local, heads_per_kv, 1)
    attended = finish(carry_state) + gate_factor * finish(image_carry_state)
    return attended.reshape(2, seq_rows, heads_local * HEAD_SIZE).astype(jnp.bfloat16)


MASKED = -1e30
EXP2_SCALE = math.log2(math.e) / math.sqrt(HEAD_SIZE)
VMEM_SPEC = pl.BlockSpec(memory_space=pltpu.VMEM)
ANY_SPEC = pl.BlockSpec(memory_space=pl.ANY)
BLOCKS = 8
CHUNK = 8
KERNEL = pltpu.CompilerParams(vmem_limit_bytes=12 << 20)


def in_vmem(*arrays):
    return [pltpu.with_memory_space_constraint(array, pltpu.VMEM) for array in arrays]


def rows_by_rows(left, right):
    return lax.dot_general(left, right, (((1,), (1,)), ((), ())), preferred_element_type=jnp.float32)


def columns_by_columns(left, right):
    return lax.dot_general(left, right, (((0,), (0,)), ((), ())), preferred_element_type=jnp.float32)


def block_of(place):
    return jnp.where(place < BLOCKS // 2, place, 3 * BLOCKS // 2 - 1 - place)


def ring_blocks(shifts):
    ctx, section = lax.axis_index("ctx"), lax.axis_index("section")
    place = jnp.where(ctx == 0, section, BLOCKS - 1 - section)
    return [block_of((place + shift + BLOCKS) & (BLOCKS - 1)) for shift in shifts], ctx * (BLOCKS // 2) + section


def position_bias(block, own, limit, rows, diagonal):
    key = lax.broadcasted_iota(jnp.int32, (rows, rows), 0)
    first = jnp.where(block <= own, block * rows, 1 << 30)
    allowed = first + key < limit
    if diagonal:
        allowed &= key <= lax.broadcasted_iota(jnp.int32, (rows, rows), 1)
    return jnp.where(allowed, 0.0, MASKED)


def weigh(scores, biases, rows, old):
    if biases:
        scores = jnp.concatenate([scores[i * rows : (i + 1) * rows] + bias for i, bias in enumerate(biases)], 0)
    best = jnp.max(scores, axis=0, keepdims=True)
    if old is not None:
        best = jnp.maximum(old, best)
    weights = jnp.exp2((scores - best) * EXP2_SCALE)
    return best, jnp.sum(weights, axis=0, keepdims=True), weights.astype(jnp.bfloat16)


def weigh_heads(scores, biases, rows, heads, old):
    parts = []
    for h in range(heads):
        part = slice(h * rows, (h + 1) * rows)
        parts.append(weigh(scores[:, part], biases, rows, None if old is None else old[:, part]))
    return [jnp.concatenate(x, 1) for x in zip(*parts)]


def in_turn(units, score, weigh_unit, collect):
    ahead = score(*units[0])
    waiting = None
    for i, unit in enumerate(units):
        scores = ahead
        if i + 1 < len(units):
            ahead = score(*units[i + 1])
        weighed = weigh_unit(*unit, scores)
        if waiting is not None:
            collect(*waiting)
        waiting = (*unit, *weighed)
    collect(*waiting)


class Heads:
    def __init__(self, q_ref, groups):
        self.q_ref = q_ref
        self.sequences, self.rows = q_ref.shape[:2]
        self.heads = q_ref.shape[2] // HEAD_SIZE // groups
        self.chunk = min(CHUNK, self.heads)
        self.units = [
            (sequence, group, h)
            for group in range(groups)
            for sequence in range(self.sequences)
            for h in range(0, self.heads, self.chunk)
        ]

    def queries(self, sequence, group, h):
        first = (group * self.heads + h) * HEAD_SIZE
        columns = [slice(first + j * HEAD_SIZE, first + (j + 1) * HEAD_SIZE) for j in range(self.chunk)]
        return jnp.concatenate([self.q_ref[sequence, :, c] for c in columns], 0)

    def part(self, h):
        return slice(h * self.rows, (h + self.chunk) * self.rows)


def key_columns(group):
    return slice(2 * group * HEAD_SIZE, (2 * group + 1) * HEAD_SIZE)


def value_columns(group):
    return slice((2 * group + 1) * HEAD_SIZE, (2 * group + 2) * HEAD_SIZE)


def stack_rows(refs, sequence, columns):
    rows = [r[sequence if r.shape[0] > 1 else 0, :, columns] for r in refs]
    return jnp.concatenate(rows, 0) if len(rows) > 1 else rows[0]


def fold(heads, length_ref, blocks, numbers, own, old_state, state):
    stat_ref, sum_ref = state
    rows = heads.rows
    biases = [
        [
            position_bias(number, own, length_ref[i : i + 1], rows, old_state is None and j == 0)
            for j, number in enumerate(numbers)
        ]
        for i in range(heads.sequences)
    ]

    def score(sequence, group, h):
        return rows_by_rows(stack_rows(blocks, sequence, key_columns(group)), heads.queries(sequence, group, h))

    def weigh_unit(sequence, group, h, scores):
        part = heads.part(h)
        old = None if old_state is None else stat_ref[sequence, group, 0:1, part]
        best, total, weights = weigh_heads(scores, biases[sequence], rows, heads.chunk, old)
        shrink = None
        if old is not None:
            shrink = jnp.exp2((old - best) * EXP2_SCALE)
            total = stat_ref[sequence, group, 1:2, part] * shrink + total
        stat_ref[sequence, group, 0:1, part] = best
        stat_ref[sequence, group, 1:2, part] = total
        return shrink, weights

    def collect(sequence, group, h, shrink, weights):
        part = heads.part(h)
        added = columns_by_columns(stack_rows(blocks, sequence, value_columns(group)), weights)
        if shrink is not None:
            added = sum_ref[sequence, group, :, part] * shrink + added
        sum_ref[sequence, group, :, part] = added

    in_turn(heads.units, score, weigh_unit, collect)


def fold_useful(heads, length_ref, blocks, numbers, own, old_state, state):
    ahead = len(blocks) - 2
    useful = [number < own for number in numbers[ahead:]]

    def work(*chosen):
        chosen = [*range(ahead), *(ahead + i for i in chosen)]
        fold(heads, length_ref, [blocks[i] for i in chosen], [numbers[i] for i in chosen], own, old_state, state)

    pl.when(useful[0] & useful[1])(lambda: work(0, 1))
    pl.when(useful[1] & ~useful[0])(lambda: work(1))
    one = useful[0] | ~useful[1] if ahead else useful[0]
    pl.when(one & ~useful[1])(lambda: work(0))


def fold_kernel(first, shifts, groups, length_ref, q_ref, *refs):
    blocks = refs[: len(shifts)]
    numbers, own = ring_blocks(shifts)
    heads = Heads(q_ref, groups)
    fold_useful(heads, length_ref, blocks, numbers, own, None if first else refs[-4:-2], refs[-2:])


def state_shapes(q, groups):
    sequences, rows, columns = q.shape
    width = columns // HEAD_SIZE // groups * rows
    return [
        pltpu.VMEM((sequences, groups, 2, width), jnp.float32),
        pltpu.VMEM((sequences, groups, HEAD_SIZE, width), jnp.float32),
    ]


def cost(q, keys):
    work = q.shape[0] * q.shape[2] // HEAD_SIZE * q.shape[1] * keys
    return pl.CostEstimate(flops=work * 4 * HEAD_SIZE, bytes_accessed=1 << 20, transcendentals=work)


def fold_blocks(lengths, q, blocks, shifts, state):
    groups = blocks[0].shape[2] // (2 * HEAD_SIZE)
    first = state is None
    state = () if first else tuple(state)
    held = 2 + len(blocks)
    return pl.pallas_call(
        functools.partial(fold_kernel, first, shifts, groups),
        in_specs=[VMEM_SPEC] * (held + len(state)),
        out_specs=[VMEM_SPEC] * 2,
        out_shape=state_shapes(q, groups),
        input_output_aliases={} if first else {held + i: i for i in range(2)},
        compiler_params=KERNEL,
        cost_estimate=cost(q, q.shape[1] * len(blocks)),
        name="fold_blocks",
    )(*in_vmem(lengths, q, *blocks, *state))


def cross_kernel(groups, factor_ref, q_ref, *refs):
    images, cross_ref = refs[:-1], refs[-1]
    heads = Heads(q_ref, groups)
    rows = heads.rows
    first = lax.axis_index("tp") * 2 * groups
    columns = [pl.ds(pl.multiple_of((first + i) * HEAD_SIZE, HEAD_SIZE), HEAD_SIZE) for i in range(2 * groups)]
    image = [jnp.concatenate([r[:, c] for r in images], 0) for c in columns]

    def score(sequence, group, h):
        return rows_by_rows(image[2 * group], heads.queries(sequence, group, h))

    def weigh_unit(sequence, group, h, scores):
        _, total, weights = weigh_heads(scores, [], rows, heads.chunk, None)
        first = group * heads.heads + h
        factors = jnp.concatenate([factor_ref[first + j : first + j + 1] for j in range(heads.chunk)], 1)
        return factors / total, weights

    def collect(sequence, group, h, factors, weights):
        cross_ref[sequence, group, :, heads.part(h)] = columns_by_columns(image[2 * group + 1], weights) * factors

    in_turn(heads.units, score, weigh_unit, collect)


def cross_attend(factors, q, images, groups):
    return pl.pallas_call(
        functools.partial(cross_kernel, groups),
        in_specs=[VMEM_SPEC] * (2 + len(images)),
        out_specs=VMEM_SPEC,
        out_shape=state_shapes(q, groups)[1],
        compiler_params=KERNEL,
        cost_estimate=cost(q, q.shape[1]),
        name="cross_attend",
    )(*in_vmem(factors, q, *images))


def turned(out, rows):
    heads = [out[:, first : first + rows].T for first in range(0, out.shape[1], rows)]
    return jnp.concatenate(heads, 1).astype(jnp.bfloat16)


class Results:
    def __init__(self, heads, out_ref, held_ref, sems):
        self.heads, self.out_ref, self.held_ref, self.sems = heads, out_ref, held_ref, sems
        self.copies = []

    def put(self, sequence, group, h, out):
        heads = self.heads
        first = (group * heads.heads + h) * HEAD_SIZE
        self.held_ref[sequence, :, first : first + heads.chunk * HEAD_SIZE] = turned(out, heads.rows)
        if h + heads.chunk == heads.heads:
            width = heads.heads * HEAD_SIZE
            at = (sequence, slice(None), pl.ds(group * width, width))
            self.send(self.held_ref.at[at], at, self.sems.at[sequence, group])

    def send(self, source, at, sem):
        copy = pltpu.make_async_copy(source, self.out_ref.at[at], sem)
        copy.start()
        self.copies.append(copy)

    def wait(self):
        for copy in self.copies:
            copy.wait()


def result_scratch(q, groups):
    return [pltpu.VMEM(q.shape, q.dtype), pltpu.SemaphoreType.DMA((q.shape[0], groups))]


def early_kernel(last_shift, groups, q_ref, cross_ref, stat_ref, sum_ref, out_ref, held_ref, sems):
    (last,), own = ring_blocks([last_shift])
    heads = Heads(q_ref, groups)

    def write():
        results = Results(heads, out_ref, held_ref, sems)
        for sequence, group, h in heads.units:
            part = heads.part(h)
            over = 1.0 / stat_ref[sequence, group, 1:2, part]
            results.put(
                sequence, group, h, sum_ref[sequence, group, :, part] * over + cross_ref[sequence, group, :, part]
            )
        results.wait()

    pl.when(last > own)(write)


def early_rows(q, last_shift, groups, cross, state):
    args = in_vmem(q, cross, *state)
    return pl.pallas_call(
        functools.partial(early_kernel, last_shift, groups),
        in_specs=[VMEM_SPEC] * len(args),
        out_specs=ANY_SPEC,
        out_shape=pltpu.HBM(q.shape, q.dtype),
        scratch_shapes=result_scratch(q, groups),
        compiler_params=KERNEL,
        cost_estimate=cost(q, q.shape[1] // 4),
        name="early_rows",
    )(*args)


def last_block(heads, sequence, shift, length_ref, block, cross_ref, stat_ref, sum_ref, put):
    rows = heads.rows
    (number,), own = ring_blocks([shift])
    biases = [position_bias(number, own, length_ref[sequence : sequence + 1], rows, False)]

    def score(sequence, group, h):
        return rows_by_rows(block[0, :, key_columns(group)], heads.queries(sequence, group, h))

    def weigh_unit(sequence, group, h, scores):
        part = heads.part(h)
        old = stat_ref[sequence, group, 0:1, part]
        best, total, weights = weigh_heads(scores, biases, rows, heads.chunk, old)
        shrink = jnp.exp2((old - best) * EXP2_SCALE)
        over = 1.0 / (stat_ref[sequence, group, 1:2, part] * shrink + total)
        return shrink * over, over, weights

    def collect(sequence, group, h, old_factor, factor, weights):
        part = heads.part(h)
        added = columns_by_columns(block[0, :, value_columns(group)], weights)
        out = sum_ref[sequence, group, :, part] * old_factor + added * factor + cross_ref[sequence, group, :, part]
        put(sequence, group, h, out)

    in_turn([unit for unit in heads.units if unit[0] == sequence], score, weigh_unit, collect)


def first_finish_kernel(shift, groups, length_ref, q_ref, block, cross_ref, stat_ref, sum_ref, rows_ref):
    heads = Heads(q_ref, groups)
    (number,), own = ring_blocks([shift])

    def put(sequence, group, h, out):
        first = (group * heads.heads + h) * HEAD_SIZE
        rows_ref[:, first : first + heads.chunk * HEAD_SIZE] = turned(out, heads.rows)

    pl.when(number < own)(
        lambda: last_block(heads, 0, shift, length_ref, block, cross_ref, stat_ref, sum_ref, put)
    )


def first_finish(lengths, q, shift, block, cross, state):
    groups = block.shape[2] // (2 * HEAD_SIZE)
    args = in_vmem(lengths, q, block, cross, *state)
    return pl.pallas_call(
        functools.partial(first_finish_kernel, shift, groups),
        in_specs=[VMEM_SPEC] * len(args),
        out_specs=VMEM_SPEC,
        out_shape=pltpu.VMEM(q.shape[1:], q.dtype),
        compiler_params=KERNEL,
        cost_estimate=cost(q, q.shape[1] // 2),
        name="first_finish",
    )(*args)


def second_finish_kernel(
    shift, groups, length_ref, q_ref, block, cross_ref, stat_ref, sum_ref, rows_ref, _, out_ref, held_ref, sems
):
    heads = Heads(q_ref, groups)
    (number,), own = ring_blocks([shift])

    def work():
        results = Results(heads, out_ref, held_ref, sems)
        results.send(rows_ref, 0, sems.at[0, 0])
        last_block(heads, 1, shift, length_ref, block, cross_ref, stat_ref, sum_ref, results.put)
        results.wait()

    pl.when(number < own)(work)


def second_finish(lengths, q, shift, block, cross, state, first_rows, result):
    groups = block.shape[2] // (2 * HEAD_SIZE)
    args = in_vmem(lengths, q, block, cross, *state, first_rows)
    return pl.pallas_call(
        functools.partial(second_finish_kernel, shift, groups),
        in_specs=[VMEM_SPEC] * len(args) + [ANY_SPEC],
        out_specs=ANY_SPEC,
        out_shape=pltpu.HBM(q.shape, q.dtype),
        scratch_shapes=result_scratch(q, groups),
        input_output_aliases={len(args): 0},
        compiler_params=KERNEL,
        cost_estimate=cost(q, q.shape[1] // 2),
        name="second_finish",
    )(*args, result)


def load_kernel(parity, *refs):
    limit_ref, factor_ref, q_out, image_out, counts, gates, sems = refs[-7:]
    lengths, gate, q_ref, image_ref = refs[:4]

    def work():
        pairs = ((lengths, counts), (gate, gates), (q_ref, q_out), (image_ref, image_out))
        copies = [pltpu.make_async_copy(source, target, sems.at[i]) for i, (source, target) in enumerate(pairs)]
        for copy in copies:
            copy.start()
        copies[0].wait()
        for i in range(limit_ref.shape[0]):
            limit_ref[i : i + 1] = jnp.full((1, limit_ref.shape[1]), counts[i], jnp.int32)
        copies[1].wait()
        for i in range(factor_ref.shape[0]):
            factor_ref[i : i + 1] = jnp.full((1, factor_ref.shape[1]), gates[i], jnp.float32)
        factor_ref[...] = jnp.tanh(factor_ref[...])
        copies[2].wait()
        copies[3].wait()

    own = None
    if parity == 0:
        kv_ref, own_ref = refs[4:6]
        width = own_ref.shape[2]
        columns = pl.ds(pl.multiple_of(lax.axis_index("tp") * width, width), width)
        own = pltpu.make_async_copy(kv_ref.at[:, :, columns], own_ref, sems.at[4])
        own.start()
    pl.when((lax.axis_index("tp") & 1) == parity)(work)
    if own is not None:
        own.wait()


def load_inputs(parity, loaded, *arrays):
    lengths, gate, q, image = arrays[:4]
    rows = q.shape[1]
    shapes = [
        pltpu.VMEM((lengths.shape[0], rows), jnp.int32),
        pltpu.VMEM((gate.shape[0], rows), jnp.float32),
        pltpu.VMEM(q.shape, q.dtype),
        pltpu.VMEM(image.shape, image.dtype),
    ]
    if parity == 0:
        kv = arrays[4]
        shapes = [pltpu.VMEM((*kv.shape[:2], kv.shape[2] // lax.axis_size("tp")), kv.dtype)] + shapes
    return pl.pallas_call(
        functools.partial(load_kernel, parity),
        in_specs=[ANY_SPEC] * len(arrays) + [VMEM_SPEC] * len(loaded),
        out_specs=[VMEM_SPEC] * len(shapes),
        out_shape=shapes,
        scratch_shapes=[
            pltpu.SMEM(lengths.shape, lengths.dtype),
            pltpu.SMEM(gate.shape, gate.dtype),
            pltpu.SemaphoreType.DMA((5,)),
        ],
        input_output_aliases={len(arrays) + i: i for i in range(len(loaded))},
        compiler_params=KERNEL,
        name="load_inputs",
    )(*[pltpu.with_memory_space_constraint(array, pltpu.HBM) for array in arrays], *in_vmem(*loaded))


def join_kernel(first_ref, second_ref, joined_ref):
    rows = [r[...].astype(jnp.float32) for r in (first_ref, second_ref)]
    joined_ref[...] = jnp.concatenate(rows, 0).astype(joined_ref.dtype)


def joined(first, second):
    return pl.pallas_call(
        join_kernel,
        in_specs=[VMEM_SPEC] * 2,
        out_specs=VMEM_SPEC,
        out_shape=pltpu.VMEM((first.shape[0] + second.shape[0], first.shape[1]), first.dtype),
        compiler_params=KERNEL,
        name="joined",
    )(*in_vmem(first, second))


def half_kernel(sequence, block_ref, half_ref):
    half_ref[...] = block_ref[sequence : sequence + 1]


def half_of(block, sequence):
    return pl.pallas_call(
        functools.partial(half_kernel, sequence),
        in_specs=[VMEM_SPEC],
        out_specs=VMEM_SPEC,
        out_shape=pltpu.VMEM((1,) + block.shape[1:], block.dtype),
        compiler_params=KERNEL,
        name="half_of",
    )(*in_vmem(block))


RING = (0, 1, 2, 3, 7, 6, 5, 4)


def ring_forward(block):
    pairs = [(RING[i], RING[(i + 1) % BLOCKS]) for i in range(BLOCKS)]
    return lax.ppermute(block, ("ctx", "section"), pairs)


def ring_backward(block):
    pairs = [(RING[(i + 1) % BLOCKS], RING[i]) for i in range(BLOCKS)]
    return lax.ppermute(block, ("ctx", "section"), pairs)


def after(block, *others):
    return lax.optimization_barrier((block,) + others)[0]


def swapped(rows, name, bits):
    return lax.ppermute(rows, name, [(i, i ^ bits) for i in range(lax.axis_size(name))])


def ring_device(queries, self_kv, image_kv, cross_gate, lengths):
    tp_count = lax.axis_size("tp")
    groups = KVH // tp_count
    own, *loaded = load_inputs(0, (), lengths, cross_gate, queries, image_kv, self_kv)
    f1, b1 = ring_forward(own), ring_backward(own)
    sections = lax.axis_size("section")
    n2 = swapped(image_kv, "ctx", 1)
    n1 = swapped(image_kv, "section", 2)
    n3 = swapped(image_kv, ("ctx", "section"), sections + 2)
    limits, factors, q, image1 = load_inputs(1, tuple(loaded), lengths, cross_gate, queries, image_kv)

    f2, b2 = ring_forward(f1), ring_backward(b1)
    image4 = jnp.concatenate([image1, n1, n2, n3], 0)
    far = swapped(image4, "section", 1)
    state = fold_blocks(limits, q, [own, f1, after(b1, image4)], (0, -1, 1), None)

    f3, b3 = ring_forward(after(f2, state[0])), ring_backward(after(b2, state[0], far))
    image8 = joined(image4, far)
    images = [image8] + [swapped(image8, "tp", bits) for bits in range(1, tp_count)]
    state = fold_blocks(limits, q, [f2, after(b2, image8)], (-2, 2), state)

    f4 = ring_forward(half_of(after(f3, state[0]), 0))
    b4 = ring_backward(half_of(after(b3, state[0], *images), 1))
    cross = cross_attend(factors, q, images, groups)
    state = fold_blocks(limits, q, [f3, b3], (-3, 3), state)
    result = early_rows(q, 4, groups, cross, state)
    first_rows = first_finish(limits, q, 4, f4, cross, state)
    return second_finish(limits, q, 4, b4, cross, state, first_rows, result)


def solution(mesh):
    placed = (
        P(None, ("ctx", "section"), "tp"),
        P(None, ("ctx", "section"), None),
        P(("ctx", "tp", "section"), None),
        P("tp"),
        P(),
    )
    ring = mesh.shape["ctx"] == 2 and mesh.shape["section"] == 4 and mesh.shape["tp"] == 4
    return jax.shard_map(
        ring_device if ring else scan_device,
        mesh=mesh,
        in_specs=placed,
        out_specs=P(None, ("ctx", "section"), "tp"),
        check_vma=False,
    )
```

```python
import functools
import math

import jax
import jax.numpy as jnp
from jax import lax
from jax.experimental import pallas as pl
from jax.experimental.pallas import tpu as pltpu
from jax.sharding import PartitionSpec as P

HQ = 64
KVH = 8
HEAD_SIZE = 128


neg_large = -1e30


def fold_block(carry_state, query_grid, key_matrix, value_matrix, allowed, score_form, value_form):
    row_best, row_total, weighted = carry_state
    logit_scores = jnp.einsum(
        score_form, query_grid, key_matrix, preferred_element_type=jnp.float32
    ) * (1.0 / math.sqrt(HEAD_SIZE))
    masked = jnp.where(allowed, logit_scores, neg_large)
    new_best = jnp.maximum(row_best, jnp.max(masked, axis=-1))
    weights = jnp.where(allowed, jnp.exp(masked - new_best[..., None]), 0.0)
    shrink = jnp.exp(row_best - new_best)
    row_total = row_total * shrink + jnp.sum(weights, axis=-1)
    weighted = weighted * shrink[..., None] + jnp.einsum(
        value_form, weights.astype(jnp.bfloat16), value_matrix, preferred_element_type=jnp.float32
    )
    return (new_best, row_total, weighted)


def finish(carry_state):
    return jnp.transpose(carry_state[2] / carry_state[1][..., None], (0, 3, 1, 2, 4))


def scan_device(queries, self_kv, image_kv, cross_gate, lengths):
    tp_count = lax.axis_size("tp")
    heads_local = HQ // tp_count
    kv_local = max(1, KVH // tp_count)
    replicas = max(1, tp_count // KVH)
    heads_per_kv = heads_local // kv_local
    seq_rows = queries.shape[1]
    kv_cols = kv_local * 2 * HEAD_SIZE
    tp_rank = lax.axis_index("tp")
    own_pairs = lax.dynamic_slice_in_dim(self_kv, tp_rank // replicas * kv_cols, kv_cols, 2)
    query_grid = queries.reshape(2, seq_rows, kv_local, heads_per_kv, HEAD_SIZE)
    block_rank = lax.axis_index(("ctx", "section"))
    query_pos = block_rank * seq_rows + jnp.arange(seq_rows, dtype=jnp.int32)
    last_needed = jnp.minimum(block_rank * seq_rows + seq_rows - 1, jnp.max(lengths) - 1)
    start_state = (
        jnp.full((2, kv_local, heads_per_kv, seq_rows), neg_large, jnp.float32),
        jnp.zeros((2, kv_local, heads_per_kv, seq_rows), jnp.float32),
        jnp.zeros((2, kv_local, heads_per_kv, seq_rows, HEAD_SIZE), jnp.float32),
    )
    carry_state = start_state
    kv_piece = lax.all_gather(own_pairs, ("ctx", "section"), axis=1, tiled=True)
    row_count = kv_piece.shape[1]
    block_rows = math.gcd(row_count, 512)
    blocks = jnp.moveaxis(
        kv_piece.reshape(2, row_count // block_rows, block_rows, kv_local, 2, HEAD_SIZE), 1, 0
    )

    def self_one_block(inner_state, scan_item):
        block_number, block_pairs = scan_item
        block_first = block_number * block_rows
        key_pos = block_first + jnp.arange(block_rows, dtype=jnp.int32)
        allowed = (key_pos[None, None, :] <= query_pos[None, :, None]) & (
            key_pos[None, None, :] < lengths[:, None, None]
        )

        def compute_block(state_in):
            return fold_block(
                state_in,
                query_grid,
                block_pairs[:, :, :, 0],
                block_pairs[:, :, :, 1],
                allowed[:, None, None],
                "bsgrd,bpgd->bgrsp",
                "bgrsp,bpgd->bgrsd",
            )

        def keep_state(state_in):
            return state_in

        return (lax.cond(block_first > last_needed, keep_state, compute_block, inner_state), None)

    carry_state, _ = lax.scan(
        self_one_block, carry_state, (jnp.arange(row_count // block_rows, dtype=jnp.int32), blocks)
    )
    image_rows = image_kv.shape[0]
    copies = jnp.repeat(image_kv.reshape(image_rows, KVH // kv_local, kv_cols), replicas, axis=1)
    image_own = lax.all_to_all(
        copies.reshape(image_rows, tp_count * kv_cols),
        "tp",
        split_axis=1,
        concat_axis=0,
        tiled=True,
    )
    image_carry_state = start_state
    kv_piece = lax.all_gather(image_own, ("ctx", "section"), axis=0, tiled=True)
    row_count = kv_piece.shape[0]
    image_block_rows = math.gcd(row_count, 512)
    blocks = kv_piece.reshape(
        row_count // image_block_rows, image_block_rows, kv_local, 2, HEAD_SIZE
    )
    everywhere = jnp.ones((), jnp.bool_)

    def image_one_block(inner_state, block_pairs):
        return (
            fold_block(
                inner_state,
                query_grid,
                block_pairs[:, :, 0],
                block_pairs[:, :, 1],
                everywhere,
                "bsgrd,pgd->bgrsp",
                "bgrsp,pgd->bgrsd",
            ),
            None,
        )

    image_carry_state, _ = lax.scan(image_one_block, image_carry_state, blocks)
    gate_factor = jnp.tanh(cross_gate).reshape(1, 1, kv_local, heads_per_kv, 1)
    attended = finish(carry_state) + gate_factor * finish(image_carry_state)
    return attended.reshape(2, seq_rows, heads_local * HEAD_SIZE).astype(jnp.bfloat16)


MASKED = -1e30
EXP2_SCALE = math.log2(math.e) / math.sqrt(HEAD_SIZE)
VMEM_SPEC = pl.BlockSpec(memory_space=pltpu.VMEM)
ANY_SPEC = pl.BlockSpec(memory_space=pl.ANY)
BLOCKS = 8
CHUNK = 8
KERNEL = pltpu.CompilerParams(vmem_limit_bytes=12 << 20)


def in_vmem(*arrays):
    return [pltpu.with_memory_space_constraint(array, pltpu.VMEM) for array in arrays]


def rows_by_rows(left, right):
    return lax.dot_general(left, right, (((1,), (1,)), ((), ())), preferred_element_type=jnp.float32)


def columns_by_columns(left, right):
    return lax.dot_general(left, right, (((0,), (0,)), ((), ())), preferred_element_type=jnp.float32)


def block_of(place):
    return jnp.where(place < BLOCKS // 2, place, 3 * BLOCKS // 2 - 1 - place)


def ring_blocks(shifts):
    ctx, section = lax.axis_index("ctx"), lax.axis_index("section")
    place = jnp.where(ctx == 0, section, BLOCKS - 1 - section)
    return [block_of((place + shift + BLOCKS) & (BLOCKS - 1)) for shift in shifts], ctx * (BLOCKS // 2) + section


def position_bias(block, own, limit, rows, diagonal):
    key = lax.broadcasted_iota(jnp.int32, (rows, rows), 0)
    first = jnp.where(block <= own, block * rows, 1 << 30)
    allowed = first + key < limit
    if diagonal:
        allowed &= key <= lax.broadcasted_iota(jnp.int32, (rows, rows), 1)
    return jnp.where(allowed, 0.0, MASKED)


def weigh(scores, biases, rows, old):
    if biases:
        scores = jnp.concatenate([scores[i * rows : (i + 1) * rows] + bias for i, bias in enumerate(biases)], 0)
    best = jnp.max(scores, axis=0, keepdims=True)
    if old is not None:
        best = jnp.maximum(old, best)
    weights = jnp.exp2((scores - best) * EXP2_SCALE)
    return best, jnp.sum(weights, axis=0, keepdims=True), weights.astype(jnp.bfloat16)


def weigh_heads(scores, biases, rows, heads, old):
    parts = []
    for h in range(heads):
        part = slice(h * rows, (h + 1) * rows)
        parts.append(weigh(scores[:, part], biases, rows, None if old is None else old[:, part]))
    return [jnp.concatenate(x, 1) for x in zip(*parts)]


def in_turn(units, score, weigh_unit, collect):
    ahead = score(*units[0])
    waiting = None
    for i, unit in enumerate(units):
        scores = ahead
        if i + 1 < len(units):
            ahead = score(*units[i + 1])
        weighed = weigh_unit(*unit, scores)
        if waiting is not None:
            collect(*waiting)
        waiting = (*unit, *weighed)
    collect(*waiting)


class Heads:
    def __init__(self, q_ref, groups):
        self.q_ref = q_ref
        self.sequences, self.rows = q_ref.shape[:2]
        self.heads = q_ref.shape[2] // HEAD_SIZE // groups
        self.chunk = min(CHUNK, self.heads)
        self.units = [
            (sequence, group, h)
            for group in range(groups)
            for sequence in range(self.sequences)
            for h in range(0, self.heads, self.chunk)
        ]

    def queries(self, sequence, group, h):
        first = (group * self.heads + h) * HEAD_SIZE
        columns = [slice(first + j * HEAD_SIZE, first + (j + 1) * HEAD_SIZE) for j in range(self.chunk)]
        return jnp.concatenate([self.q_ref[sequence, :, c] for c in columns], 0)

    def part(self, h):
        return slice(h * self.rows, (h + self.chunk) * self.rows)


def key_columns(group):
    return slice(2 * group * HEAD_SIZE, (2 * group + 1) * HEAD_SIZE)


def value_columns(group):
    return slice((2 * group + 1) * HEAD_SIZE, (2 * group + 2) * HEAD_SIZE)


def stack_rows(refs, sequence, columns):
    rows = [r[sequence if r.shape[0] > 1 else 0, :, columns] for r in refs]
    return jnp.concatenate(rows, 0) if len(rows) > 1 else rows[0]


def fold(heads, length_ref, blocks, numbers, own, old_state, state):
    stat_ref, sum_ref = state
    rows = heads.rows
    biases = [
        [
            position_bias(number, own, length_ref[i : i + 1], rows, old_state is None and j == 0)
            for j, number in enumerate(numbers)
        ]
        for i in range(heads.sequences)
    ]

    def score(sequence, group, h):
        return rows_by_rows(stack_rows(blocks, sequence, key_columns(group)), heads.queries(sequence, group, h))

    def weigh_unit(sequence, group, h, scores):
        part = heads.part(h)
        old = None if old_state is None else stat_ref[sequence, group, 0:1, part]
        best, total, weights = weigh_heads(scores, biases[sequence], rows, heads.chunk, old)
        shrink = None
        if old is not None:
            shrink = jnp.exp2((old - best) * EXP2_SCALE)
            total = stat_ref[sequence, group, 1:2, part] * shrink + total
        stat_ref[sequence, group, 0:1, part] = best
        stat_ref[sequence, group, 1:2, part] = total
        return shrink, weights

    def collect(sequence, group, h, shrink, weights):
        part = heads.part(h)
        added = columns_by_columns(stack_rows(blocks, sequence, value_columns(group)), weights)
        if shrink is not None:
            added = sum_ref[sequence, group, :, part] * shrink + added
        sum_ref[sequence, group, :, part] = added

    in_turn(heads.units, score, weigh_unit, collect)


def fold_useful(heads, length_ref, blocks, numbers, own, old_state, state):
    ahead = len(blocks) - 2
    useful = [number < own for number in numbers[ahead:]]

    def work(*chosen):
        chosen = [*range(ahead), *(ahead + i for i in chosen)]
        fold(heads, length_ref, [blocks[i] for i in chosen], [numbers[i] for i in chosen], own, old_state, state)

    pl.when(useful[0] & useful[1])(lambda: work(0, 1))
    pl.when(useful[1] & ~useful[0])(lambda: work(1))
    one = useful[0] | ~useful[1] if ahead else useful[0]
    pl.when(one & ~useful[1])(lambda: work(0))


def fold_kernel(first, shifts, groups, length_ref, q_ref, *refs):
    blocks = refs[: len(shifts)]
    numbers, own = ring_blocks(shifts)
    heads = Heads(q_ref, groups)
    fold_useful(heads, length_ref, blocks, numbers, own, None if first else refs[-4:-2], refs[-2:])


def state_shapes(q, groups):
    sequences, rows, columns = q.shape
    width = columns // HEAD_SIZE // groups * rows
    return [
        pltpu.VMEM((sequences, groups, 2, width), jnp.float32),
        pltpu.VMEM((sequences, groups, HEAD_SIZE, width), jnp.float32),
    ]


def cost(q, keys):
    work = q.shape[0] * q.shape[2] // HEAD_SIZE * q.shape[1] * keys
    return pl.CostEstimate(flops=work * 4 * HEAD_SIZE, bytes_accessed=1 << 20, transcendentals=work)


def fold_blocks(lengths, q, blocks, shifts, state):
    groups = blocks[0].shape[2] // (2 * HEAD_SIZE)
    first = state is None
    state = () if first else tuple(state)
    held = 2 + len(blocks)
    return pl.pallas_call(
        functools.partial(fold_kernel, first, shifts, groups),
        in_specs=[VMEM_SPEC] * (held + len(state)),
        out_specs=[VMEM_SPEC] * 2,
        out_shape=state_shapes(q, groups),
        input_output_aliases={} if first else {held + i: i for i in range(2)},
        compiler_params=KERNEL,
        cost_estimate=cost(q, q.shape[1] * len(blocks)),
        name="fold_blocks",
    )(*in_vmem(lengths, q, *blocks, *state))


def cross_kernel(groups, factor_ref, q_ref, *refs):
    images, cross_ref = refs[:-1], refs[-1]
    heads = Heads(q_ref, groups)
    rows = heads.rows
    first = lax.axis_index("tp") * 2 * groups
    columns = [pl.ds(pl.multiple_of((first + i) * HEAD_SIZE, HEAD_SIZE), HEAD_SIZE) for i in range(2 * groups)]
    image = [jnp.concatenate([r[:, c] for r in images], 0) for c in columns]

    def score(sequence, group, h):
        return rows_by_rows(image[2 * group], heads.queries(sequence, group, h))

    def weigh_unit(sequence, group, h, scores):
        _, total, weights = weigh_heads(scores, [], rows, heads.chunk, None)
        first = group * heads.heads + h
        factors = jnp.concatenate([factor_ref[first + j : first + j + 1] for j in range(heads.chunk)], 1)
        return factors / total, weights

    def collect(sequence, group, h, factors, weights):
        cross_ref[sequence, group, :, heads.part(h)] = columns_by_columns(image[2 * group + 1], weights) * factors

    in_turn(heads.units, score, weigh_unit, collect)


def cross_attend(factors, q, images, groups):
    return pl.pallas_call(
        functools.partial(cross_kernel, groups),
        in_specs=[VMEM_SPEC] * (2 + len(images)),
        out_specs=VMEM_SPEC,
        out_shape=state_shapes(q, groups)[1],
        compiler_params=KERNEL,
        cost_estimate=cost(q, q.shape[1]),
        name="cross_attend",
    )(*in_vmem(factors, q, *images))


def turned(out, rows):
    heads = [out[:, first : first + rows].T for first in range(0, out.shape[1], rows)]
    return jnp.concatenate(heads, 1).astype(jnp.bfloat16)


class Results:
    def __init__(self, heads, out_ref, held_ref, sems):
        self.heads, self.out_ref, self.held_ref, self.sems = heads, out_ref, held_ref, sems
        self.copies = []

    def put(self, sequence, group, h, out):
        heads = self.heads
        first = (group * heads.heads + h) * HEAD_SIZE
        self.held_ref[sequence, :, first : first + heads.chunk * HEAD_SIZE] = turned(out, heads.rows)
        if h + heads.chunk == heads.heads:
            width = heads.heads * HEAD_SIZE
            at = (sequence, slice(None), pl.ds(group * width, width))
            self.send(self.held_ref.at[at], at, self.sems.at[sequence, group])

    def send(self, source, at, sem):
        copy = pltpu.make_async_copy(source, self.out_ref.at[at], sem)
        copy.start()
        self.copies.append(copy)

    def wait(self):
        for copy in self.copies:
            copy.wait()


def result_scratch(q, groups):
    return [pltpu.VMEM(q.shape, q.dtype), pltpu.SemaphoreType.DMA((q.shape[0], groups))]


def early_kernel(last_shift, groups, q_ref, cross_ref, stat_ref, sum_ref, out_ref, held_ref, sems):
    (last,), own = ring_blocks([last_shift])
    heads = Heads(q_ref, groups)

    def write():
        results = Results(heads, out_ref, held_ref, sems)
        for sequence, group, h in heads.units:
            part = heads.part(h)
            over = 1.0 / stat_ref[sequence, group, 1:2, part]
            results.put(
                sequence, group, h, sum_ref[sequence, group, :, part] * over + cross_ref[sequence, group, :, part]
            )
        results.wait()

    pl.when(last > own)(write)


def early_rows(q, last_shift, groups, cross, state):
    args = in_vmem(q, cross, *state)
    return pl.pallas_call(
        functools.partial(early_kernel, last_shift, groups),
        in_specs=[VMEM_SPEC] * len(args),
        out_specs=ANY_SPEC,
        out_shape=pltpu.HBM(q.shape, q.dtype),
        scratch_shapes=result_scratch(q, groups),
        compiler_params=KERNEL,
        cost_estimate=cost(q, q.shape[1] // 4),
        name="early_rows",
    )(*args)


def last_block(heads, sequence, shift, length_ref, block, cross_ref, stat_ref, sum_ref, put):
    rows = heads.rows
    (number,), own = ring_blocks([shift])
    biases = [position_bias(number, own, length_ref[sequence : sequence + 1], rows, False)]

    def score(sequence, group, h):
        return rows_by_rows(block[0, :, key_columns(group)], heads.queries(sequence, group, h))

    def weigh_unit(sequence, group, h, scores):
        part = heads.part(h)
        old = stat_ref[sequence, group, 0:1, part]
        best, total, weights = weigh_heads(scores, biases, rows, heads.chunk, old)
        shrink = jnp.exp2((old - best) * EXP2_SCALE)
        over = 1.0 / (stat_ref[sequence, group, 1:2, part] * shrink + total)
        return shrink * over, over, weights

    def collect(sequence, group, h, old_factor, factor, weights):
        part = heads.part(h)
        added = columns_by_columns(block[0, :, value_columns(group)], weights)
        out = sum_ref[sequence, group, :, part] * old_factor + added * factor + cross_ref[sequence, group, :, part]
        put(sequence, group, h, out)

    in_turn([unit for unit in heads.units if unit[0] == sequence], score, weigh_unit, collect)


def first_finish_kernel(shift, groups, length_ref, q_ref, block, cross_ref, stat_ref, sum_ref, rows_ref):
    heads = Heads(q_ref, groups)
    (number,), own = ring_blocks([shift])

    def put(sequence, group, h, out):
        first = (group * heads.heads + h) * HEAD_SIZE
        rows_ref[:, first : first + heads.chunk * HEAD_SIZE] = turned(out, heads.rows)

    pl.when(number < own)(
        lambda: last_block(heads, 0, shift, length_ref, block, cross_ref, stat_ref, sum_ref, put)
    )


def first_finish(lengths, q, shift, block, cross, state):
    groups = block.shape[2] // (2 * HEAD_SIZE)
    args = in_vmem(lengths, q, block, cross, *state)
    return pl.pallas_call(
        functools.partial(first_finish_kernel, shift, groups),
        in_specs=[VMEM_SPEC] * len(args),
        out_specs=VMEM_SPEC,
        out_shape=pltpu.VMEM(q.shape[1:], q.dtype),
        compiler_params=KERNEL,
        cost_estimate=cost(q, q.shape[1] // 2),
        name="first_finish",
    )(*args)


def second_finish_kernel(
    shift, groups, length_ref, q_ref, block, cross_ref, stat_ref, sum_ref, rows_ref, _, out_ref, held_ref, sems
):
    heads = Heads(q_ref, groups)
    (number,), own = ring_blocks([shift])

    def work():
        results = Results(heads, out_ref, held_ref, sems)
        results.send(rows_ref, 0, sems.at[0, 0])
        last_block(heads, 1, shift, length_ref, block, cross_ref, stat_ref, sum_ref, results.put)
        results.wait()

    pl.when(number < own)(work)


def second_finish(lengths, q, shift, block, cross, state, first_rows, result):
    groups = block.shape[2] // (2 * HEAD_SIZE)
    args = in_vmem(lengths, q, block, cross, *state, first_rows)
    return pl.pallas_call(
        functools.partial(second_finish_kernel, shift, groups),
        in_specs=[VMEM_SPEC] * len(args) + [ANY_SPEC],
        out_specs=ANY_SPEC,
        out_shape=pltpu.HBM(q.shape, q.dtype),
        scratch_shapes=result_scratch(q, groups),
        input_output_aliases={len(args): 0},
        compiler_params=KERNEL,
        cost_estimate=cost(q, q.shape[1] // 2),
        name="second_finish",
    )(*args, result)


def load_kernel(parity, *refs):
    limit_ref, factor_ref, q_out, image_out, counts, gates, sems = refs[-7:]
    lengths, gate, q_ref, image_ref = refs[:4]

    def work():
        pairs = ((lengths, counts), (gate, gates), (q_ref, q_out), (image_ref, image_out))
        copies = [pltpu.make_async_copy(source, target, sems.at[i]) for i, (source, target) in enumerate(pairs)]
        for copy in copies:
            copy.start()
        copies[0].wait()
        for i in range(limit_ref.shape[0]):
            limit_ref[i : i + 1] = jnp.full((1, limit_ref.shape[1]), counts[i], jnp.int32)
        copies[1].wait()
        for i in range(factor_ref.shape[0]):
            factor_ref[i : i + 1] = jnp.full((1, factor_ref.shape[1]), gates[i], jnp.float32)
        factor_ref[...] = jnp.tanh(factor_ref[...])
        copies[2].wait()
        copies[3].wait()

    own = None
    if parity == 0:
        kv_ref, own_ref = refs[4:6]
        width = own_ref.shape[2]
        columns = pl.ds(pl.multiple_of(lax.axis_index("tp") * width, width), width)
        own = pltpu.make_async_copy(kv_ref.at[:, :, columns], own_ref, sems.at[4])
        own.start()
    pl.when((lax.axis_index("tp") & 1) == parity)(work)
    if own is not None:
        own.wait()


def load_inputs(parity, loaded, *arrays):
    lengths, gate, q, image = arrays[:4]
    rows = q.shape[1]
    shapes = [
        pltpu.VMEM((lengths.shape[0], rows), jnp.int32),
        pltpu.VMEM((gate.shape[0], rows), jnp.float32),
        pltpu.VMEM(q.shape, q.dtype),
        pltpu.VMEM(image.shape, image.dtype),
    ]
    if parity == 0:
        kv = arrays[4]
        shapes = [pltpu.VMEM((*kv.shape[:2], kv.shape[2] // lax.axis_size("tp")), kv.dtype)] + shapes
    return pl.pallas_call(
        functools.partial(load_kernel, parity),
        in_specs=[ANY_SPEC] * len(arrays) + [VMEM_SPEC] * len(loaded),
        out_specs=[VMEM_SPEC] * len(shapes),
        out_shape=shapes,
        scratch_shapes=[
            pltpu.SMEM(lengths.shape, lengths.dtype),
            pltpu.SMEM(gate.shape, gate.dtype),
            pltpu.SemaphoreType.DMA((5,)),
        ],
        input_output_aliases={len(arrays) + i: i for i in range(len(loaded))},
        compiler_params=KERNEL,
        name="load_inputs",
    )(*[pltpu.with_memory_space_constraint(array, pltpu.HBM) for array in arrays], *in_vmem(*loaded))


def join_kernel(first_ref, second_ref, joined_ref):
    rows = [r[...].astype(jnp.float32) for r in (first_ref, second_ref)]
    joined_ref[...] = jnp.concatenate(rows, 0).astype(joined_ref.dtype)


def joined(first, second):
    return pl.pallas_call(
        join_kernel,
        in_specs=[VMEM_SPEC] * 2,
        out_specs=VMEM_SPEC,
        out_shape=pltpu.VMEM((first.shape[0] + second.shape[0], first.shape[1]), first.dtype),
        compiler_params=KERNEL,
        name="joined",
    )(*in_vmem(first, second))


def half_kernel(sequence, block_ref, half_ref):
    half_ref[...] = block_ref[sequence : sequence + 1]


def half_of(block, sequence):
    return pl.pallas_call(
        functools.partial(half_kernel, sequence),
        in_specs=[VMEM_SPEC],
        out_specs=VMEM_SPEC,
        out_shape=pltpu.VMEM((1,) + block.shape[1:], block.dtype),
        compiler_params=KERNEL,
        name="half_of",
    )(*in_vmem(block))


RING = (0, 1, 2, 3, 7, 6, 5, 4)


def ring_forward(block):
    pairs = [(RING[i], RING[(i + 1) % BLOCKS]) for i in range(BLOCKS)]
    return lax.ppermute(block, ("ctx", "section"), pairs)


def ring_backward(block):
    pairs = [(RING[(i + 1) % BLOCKS], RING[i]) for i in range(BLOCKS)]
    return lax.ppermute(block, ("ctx", "section"), pairs)


def after(block, *others):
    return lax.optimization_barrier((block,) + others)[0]


def swapped(rows, name, bits):
    return lax.ppermute(rows, name, [(i, i ^ bits) for i in range(lax.axis_size(name))])


def ring_device(queries, self_kv, image_kv, cross_gate, lengths):
    tp_count = lax.axis_size("tp")
    groups = KVH // tp_count
    own, *loaded = load_inputs(0, (), lengths, cross_gate, queries, image_kv, self_kv)
    f1, b1 = ring_forward(own), ring_backward(own)
    sections = lax.axis_size("section")
    n2 = swapped(image_kv, "ctx", 1)
    n1 = swapped(image_kv, "section", 2)
    n3 = swapped(image_kv, ("ctx", "section"), sections + 2)
    limits, factors, q, image1 = load_inputs(1, tuple(loaded), lengths, cross_gate, queries, image_kv)

    f2, b2 = ring_forward(f1), ring_backward(b1)
    image4 = jnp.concatenate([image1, n1, n2, n3], 0)
    far = swapped(image4, "section", 1)
    state = fold_blocks(limits, q, [own, f1, after(b1, image4)], (0, -1, 1), None)

    f3, b3 = ring_forward(after(f2, state[0])), ring_backward(after(b2, state[0], far))
    image8 = joined(image4, far)
    images = [image8] + [swapped(image8, "tp", bits) for bits in range(1, tp_count)]
    state = fold_blocks(limits, q, [f2, b2], (-2, 2), state)

    f4 = ring_forward(half_of(after(f3, state[0]), 0))
    b4 = ring_backward(half_of(after(b3, state[0], *images), 1))
    cross = cross_attend(factors, q, images, groups)
    state = fold_blocks(limits, q, [f3, b3], (-3, 3), state)
    result = early_rows(q, 4, groups, cross, state)
    first_rows = first_finish(limits, q, 4, f4, cross, state)
    return second_finish(limits, q, 4, b4, cross, state, first_rows, result)


def solution(mesh):
    placed = (
        P(None, ("ctx", "section"), "tp"),
        P(None, ("ctx", "section"), None),
        P(("ctx", "tp", "section"), None),
        P("tp"),
        P(),
    )
    ring = mesh.shape["ctx"] == 2 and mesh.shape["section"] == 4 and mesh.shape["tp"] == 4
    return jax.shard_map(
        ring_device if ring else scan_device,
        mesh=mesh,
        in_specs=placed,
        out_specs=P(None, ("ctx", "section"), "tp"),
        check_vma=False,
    )
```
